32 devices in a mesh: row: 4 (over z), col: 2 (over x), depth: 4 (over y, core).
Axes of the slice: x: 2, y: 2, z: 4, core: 2. Of those that a mesh axis runs over, the one named last changes fastest.
Arguments:
- density: bfloat16 [2048, 2048], P('row', 'col'), as said below
Outputs:
- purified: float32 [2048, 2048], P('row', ('col', 'depth'))
Inputs may be any that keep to these rules, and one draw needn't show every extreme that they name: density is symmetric: density[i, j] == density[j, i] for every i and j, for any seed.
All inputs are finite; a program needn't handle non-finite values.
Results may differ from the reference program's by a relative error of at most 0.002.
Values may be sent and summed in bfloat16 or wider, within the bound.
No kernel may reach another device: no remote copies, remote signals or barrier semaphores. Data moves between devices by JAX's collectives and lax.ppermute only.
A program may use at most 64 MiB of HBM per device.

```python
import jax
import jax.numpy as jnp

N = 2048


def draw_density(key, part):
    base_key = jax.random.fold_in(key, 11)
    entries = jax.random.normal(base_key, (N, N), jnp.float32) * 0.0707107
    symmetric = 0.5 * (entries + entries.T)
    return jnp.clip(symmetric, -0.35, 0.35).astype(jnp.bfloat16)


def setup_inputs(seed: int = 0) -> dict:
    splits = jax.random.split(jax.random.key(seed), 2)
    return {
        "density": draw_density(jax.random.fold_in(splits[1], 71), 0),
    }


def reference(density):
    square = jnp.dot(density, density, preferred_element_type=jnp.float32).astype(jnp.bfloat16)
    cube_sum = jnp.dot(square, density, preferred_element_type=jnp.float32)
    return 3.0 * square.astype(jnp.float32) - 2.0 * cube_sum
```

```python
import functools

import jax
import jax.numpy as jnp
from jax import lax
from jax.experimental import pallas as pl
from jax.experimental.pallas import tpu as pltpu
from jax.sharding import PartitionSpec as P


def split_products(density):
    rows_blk, cols_blk = density.shape
    depth_n = lax.axis_size("depth")
    strip_len = rows_blk // depth_n
    groups = cols_blk // rows_blk
    layer_idx = lax.axis_index("depth")
    col_strips = lax.dynamic_index_in_dim(
        density.reshape(rows_blk, groups, depth_n, strip_len), layer_idx, 2, keepdims=False
    ).reshape(rows_blk, groups * strip_len)
    row_strips = lax.dynamic_index_in_dim(
        density.reshape(depth_n, strip_len, cols_blk), layer_idx, 0, keepdims=False
    )

    def gather_slab(local_slab):
        return lax.all_gather(local_slab, "col", axis=1, tiled=True)

    def multiply(left_full):
        return jnp.dot(
            left_full,
            lax.all_gather(row_strips, "row", axis=0, tiled=True),
            preferred_element_type=jnp.float32,
        )

    partial_square = multiply(gather_slab(col_strips))
    square = lax.psum(partial_square, "depth").astype(jnp.bfloat16)
    square_strips = lax.dynamic_index_in_dim(
        square.reshape(rows_blk, groups, depth_n, strip_len), layer_idx, 2, keepdims=False
    ).reshape(rows_blk, groups * strip_len)
    partial_cube = multiply(gather_slab(square_strips))
    cube_sum = lax.psum_scatter(-2.0 * partial_cube, "depth", scatter_dimension=1, tiled=True)
    share_width = cols_blk // depth_n
    own_square = lax.dynamic_slice_in_dim(square, layer_idx * share_width, share_width, 1).astype(
        jnp.float32
    )
    return cube_sum + 3.0 * own_square


def dot(a, b):
    return jnp.dot(a, b, preferred_element_type=jnp.float32)


def dot_t(a, b):
    return lax.dot_general(a, b, (((1,), (1,)), ((), ())), preferred_element_type=jnp.float32)


def place():
    z, x, d = lax.axis_index("row"), lax.axis_index("col"), lax.axis_index("depth")
    return z, x, d, lax.div(d, 2), lax.rem(d, 2)


def picked(z, x):
    return lax.rem(z, 2) ^ lax.div(z, 2) ^ x


def purify_kernel(half, own, near, far, own0, own1, own2, own3, oth0, oth1, oth2a, oth2b, oth3a, oth3b, out, row, total, square):
    z, x, d, y, c = place()
    zr = z ^ (2 * x)
    for s in range(4):
        row[s] = own[:, s * half : (s + 1) * half]
        row[4 + s, pl.ds(pl.multiple_of(c * half, half), half)] = near[:, s * half : (s + 1) * half]
        row[4 + s, pl.ds(pl.multiple_of((1 - c) * half, half), half)] = far[:, s * half : (s + 1) * half]

    def rows_of(s, h):
        return row[s, pl.ds(pl.multiple_of(h * half, half), half)]

    for s in range(8):
        total[s] = dot(row[2 * zr], row[s, :half]) + dot(row[2 * zr + 1], row[s, half:])
    for h in range(2):
        acc = total[2 * zr + h]
        for m in (1, 2, 3):
            for g in range(2):
                s = 2 * (zr ^ m) + g
                acc += dot_t(row[s], row[s, h * half : (h + 1) * half])
        total[2 * zr + h] = acc

    def blocks():
        for other in range(2):
            xx = x ^ other
            for slot, dist in enumerate((2, 1, 3)):
                src = z ^ dist
                if slot == 0:
                    i, k = src, 2 * xx + picked(src, xx)
                elif slot == 1:
                    i = k = 2 * xx + (lax.rem(z, 2) ^ 1)
                else:
                    i, k = src, 2 * xx + (1 - picked(src, xx))
                i, k = i ^ (2 * x), k ^ (2 * x)
                if other:
                    q = (
                        lambda slot=slot: oth0[slot],
                        lambda slot=slot: oth1[slot],
                        lambda slot=slot: jnp.concatenate([oth2a[slot], oth2b[slot]], 0),
                        lambda slot=slot: jnp.concatenate([oth3a[slot], oth3b[slot]], 0),
                    )
                else:
                    q = tuple((lambda r=r, slot=slot: r[slot]) for r in (own0, own1, own2, own3))
                yield slot, i, k, q

    for slot, i, k, q in blocks():
        for cc in range(2):
            total[2 * k + (c ^ cc)] += dot(row[2 * i + y], q[cc]()) + dot(row[2 * i + (1 - y)], q[2 + cc]())
        if slot != 1:

            def mirrored(i=i, k=k, q=q):
                for yy in range(2):
                    total[2 * i + (y ^ yy)] += dot_t(row[2 * k + c], q[2 * yy]()) + dot_t(
                        row[2 * k + (1 - c)], q[2 * yy + 1]()
                    )

            if slot == 0:
                pl.when(i != k)(mirrored)
            else:
                mirrored()

    for s in range(8):
        square[s] = total[s].astype(jnp.bfloat16)

    out[...] = 3.0 * square[d].astype(jnp.float32) - 2.0 * (
        dot(square[2 * zr], row[d, :half]) + dot(square[2 * zr + 1], row[d, half:])
    )

    @pl.when(zr == y)
    def _():
        acc = out[...]
        for m in (1, 2, 3):
            for g in range(2):
                s = 2 * (zr ^ m) + g
                acc -= 2.0 * dot_t(square[s], rows_of(s, c))
        out[...] = acc

    for slot, i, k, q in blocks():

        @pl.when(k == y)
        def _(i=i, q=q):
            out[...] -= 2.0 * (dot(square[2 * i + y], q[0]()) + dot(square[2 * i + (1 - y)], q[2]()))

        if slot != 1:
            for same in range(2):

                @pl.when((i == y) & (i != k) & ((y == c) if same else (y != c)))
                def _(k=k, q=q, same=same):
                    a, b = (q[0], q[1]) if same else (q[2], q[3])
                    out[...] -= 2.0 * (dot_t(square[2 * k + c], a()) + dot_t(square[2 * k + (1 - c)], b()))


def gathered(density):
    blk, half = density.shape[0], density.shape[0] // 2
    z, x, d, y, c = place()

    def by_z(v, m):
        return lax.ppermute(v, "row", [(i, i ^ m) for i in range(lax.axis_size("row"))])

    def by_x(v):
        return lax.ppermute(v, "col", [(i, i ^ 1) for i in range(lax.axis_size("col"))])

    def by_depth(v, m):
        return lax.ppermute(v, "depth", [(i, i ^ m) for i in range(lax.axis_size("depth"))])

    def quarter(k):
        return lax.dynamic_slice(density, (y * half, k * blk + c * half), (half, half))

    pick = picked(z, x)
    sent = quarter(pick)
    two_away = by_z(sent, 2)
    three_away = by_z(quarter(1 - pick), 3)
    near = by_x(lax.dynamic_slice(density, (c * half, 0), (half, 2 * blk)))
    one_away = by_z(jnp.where(lax.div(z, 2) == x, sent, two_away), 1)
    far = by_depth(near, 1)
    own0 = jnp.stack([two_away, one_away, three_away])
    oth0 = by_x(own0)
    own2 = by_depth(own0, 2)
    oth2a = by_depth(oth0[:, : half // 2], 2)
    oth2b = by_x(own2[:, half // 2 :])
    own1, oth1, own3, oth3a, oth3b = (by_depth(v, 1) for v in (own0, oth0, own2, oth2a, oth2b))
    args = (density, near, far, own0, own1, own2, own3, oth0, oth1, oth2a, oth2b, oth3a, oth3b)
    return pl.pallas_call(
        functools.partial(purify_kernel, half),
        out_shape=jax.ShapeDtypeStruct((blk, half), jnp.float32),
        in_specs=[pl.BlockSpec(memory_space=pltpu.VMEM)] * len(args),
        out_specs=pl.BlockSpec(memory_space=pltpu.VMEM),
        scratch_shapes=[
            pltpu.VMEM((8, blk, half), jnp.bfloat16),
            pltpu.VMEM((8, blk, half), jnp.float32),
            pltpu.VMEM((8, blk, half), jnp.bfloat16),
        ],
        compiler_params=pltpu.CompilerParams(vmem_limit_bytes=48 * 1024 * 1024),
        name="purify",
    )(*args)


def solution(mesh):
    four_by_two = mesh.shape["row"] == mesh.shape["depth"] == 2 * mesh.shape["col"] == 4
    return jax.shard_map(
        gathered if four_by_two else split_products,
        mesh=mesh,
        in_specs=(P("row", "col"),),
        out_specs=P("row", ("col", "depth")),
        check_vma=False,
    )
```

```python
import functools

import jax
import jax.numpy as jnp
from jax import lax
from jax.experimental import pallas as pl
from jax.experimental.pallas import tpu as pltpu
from jax.sharding import PartitionSpec as P

MIB = 1024 * 1024


def split_products(density):
    rows_blk, cols_blk = density.shape
    depth_n = lax.axis_size("depth")
    strip_len = rows_blk // depth_n
    groups = cols_blk // rows_blk
    layer_idx = lax.axis_index("depth")
    col_strips = lax.dynamic_index_in_dim(
        density.reshape(rows_blk, groups, depth_n, strip_len), layer_idx, 2, keepdims=False
    ).reshape(rows_blk, groups * strip_len)
    row_strips = lax.dynamic_index_in_dim(
        density.reshape(depth_n, strip_len, cols_blk), layer_idx, 0, keepdims=False
    )

    def gather_slab(local_slab):
        return lax.all_gather(local_slab, "col", axis=1, tiled=True)

    def multiply(left_full):
        return jnp.dot(
            left_full,
            lax.all_gather(row_strips, "row", axis=0, tiled=True),
            preferred_element_type=jnp.float32,
        )

    partial_square = multiply(gather_slab(col_strips))
    square = lax.psum(partial_square, "depth").astype(jnp.bfloat16)
    square_strips = lax.dynamic_index_in_dim(
        square.reshape(rows_blk, groups, depth_n, strip_len), layer_idx, 2, keepdims=False
    ).reshape(rows_blk, groups * strip_len)
    partial_cube = multiply(gather_slab(square_strips))
    cube_sum = lax.psum_scatter(-2.0 * partial_cube, "depth", scatter_dimension=1, tiled=True)
    share_width = cols_blk // depth_n
    own_square = lax.dynamic_slice_in_dim(square, layer_idx * share_width, share_width, 1).astype(
        jnp.float32
    )
    return cube_sum + 3.0 * own_square


def dot(a, b):
    return jnp.dot(a, b, preferred_element_type=jnp.float32)


def turned(a):
    n = a.shape[1]
    unit = lax.broadcasted_iota(jnp.int32, (n, n), 0) == lax.broadcasted_iota(jnp.int32, (n, n), 1)
    unit = unit.astype(jnp.float32).astype(a.dtype)
    return lax.dot_general(unit, a, (((1,), (1,)), ((), ())), preferred_element_type=jnp.float32).astype(a.dtype)


def place():
    z, x, d = lax.axis_index("row"), lax.axis_index("col"), lax.axis_index("depth")
    return z, x, d, lax.div(d, 2), lax.rem(d, 2)


def picked(z, x):
    return lax.rem(z, 2) ^ lax.div(z, 2) ^ x


def received(slot, other):
    z, x, _, _, _ = place()
    away = x ^ other ^ lax.div(z, 2)
    if slot == 0:
        return 2, 1 + away
    if slot == 1:
        return 1 + 2 * away, 1 + 2 * away
    return 3, 1 + away


def lanes(s, half):
    return pl.ds(pl.multiple_of(s * half, half), half)


def put(columns, i, k, quarter):
    half = quarter.shape[0]
    columns[k, lanes(i, half)] = quarter
    columns[i, lanes(k, half)] = turned(quarter)


def put_strip(columns, other, y_dist, same_core, other_core):
    _, _, _, y, c = place()
    for slot in range(3):
        i, k = received(slot, other)
        for cc, quarter in ((c, same_core(slot)), (1 - c, other_core(slot))):
            put(columns, 2 * i + (y ^ y_dist), 2 * k + cc, quarter)


def put_row(row, columns, m, rows, piece):
    half = columns.shape[2]
    for h in range(2):
        part = piece[:, h * half : (h + 1) * half]
        s = 2 * m + h
        if rows is None:
            row[:, lanes(s, half)] = part
            for g in range(2):
                put(columns, g, s, part[g * half : (g + 1) * half])
        else:
            row[lanes(rows, half), lanes(s, half)] = part
            put(columns, rows, s, part)


def home():
    z, x, _, _, _ = place()
    return (x == lax.div(z, 2)).astype(jnp.int32)


def early_halves():
    _, _, _, y, _ = place()
    at_home = home()
    return 0, 1, (4 + y) * (1 - at_home) + 2 * at_home, (6 + y) * (1 - at_home) + 3 * at_home


def late_halves():
    _, _, _, y, _ = place()
    at_home = home()
    return (
        2 + 2 * at_home,
        3 + 2 * at_home,
        (5 - y) * (1 - at_home) + (6 + y) * at_home,
        (7 - y),
    )


def slices_kernel(density, sent, half_row, third, sems):
    del sent
    z, x, _, y, c = place()
    half = third.shape[0]
    copies = (
        pltpu.make_async_copy(density.at[lanes(c, half)], half_row, sems.at[0]),
        pltpu.make_async_copy(
            density.at[lanes(y, half), lanes(2 * (1 - picked(z, x)) + c, half)], third, sems.at[1]
        ),
    )
    for copy in copies:
        copy.start()
    for copy in copies:
        copy.wait()


def row_kernel(own0, own1, near, far, own, row, columns, square):
    z, x, _, _, c = place()
    blk, half = own.shape[0], columns.shape[2]
    for b in range(2):
        put_row(row, columns, (2 * x + b) ^ z, None, own[:, b * blk : (b + 1) * blk])
    for b in range(2):
        m = (2 * (1 - x) + b) ^ z
        put_row(row, columns, m, c, near[:, b * blk : (b + 1) * blk])
        put_row(row, columns, m, 1 - c, far[:, b * blk : (b + 1) * blk])
    put_strip(columns, 0, 0, lambda s: own0[s], lambda s: own1[s])
    for s in early_halves()[:2]:
        square[:, lanes(s, half)] = dot(row[...], columns[s]).astype(square.dtype)


def middle_kernel(row, columns_in, square_in, own2, own3, oth0, oth1, columns, square, partial):
    del columns_in, square_in
    _, _, _, y, c = place()
    half = columns.shape[2]
    put_strip(columns, 0, 1, lambda s: own2[s], lambda s: own3[s])
    put_strip(columns, 1, 0, lambda s: oth0[s], lambda s: oth1[s])
    nothing = jnp.zeros((half, half), columns.dtype)
    for slot in range(3):
        i, k = received(slot, 1)
        for h in range(2):
            columns[2 * k + h, lanes(2 * i + 1 - y, half)] = nothing

            @pl.when(i != k)
            def _(i=i, k=k, h=h):
                columns[2 * i + 1 - y, lanes(2 * k + h, half)] = nothing

    for s in early_halves()[2:]:
        square[:, lanes(s, half)] = dot(row[...], columns[s]).astype(square.dtype)
    for n, s in enumerate(late_halves()):
        partial[n] = dot(row[...], columns[s])


def last_kernel(row, columns_in, square_in, partial, oth2a, oth2b, oth3a, oth3b, out, columns, square):
    del columns_in, square_in
    z, x, _, y, c = place()
    half = columns.shape[2]
    put_strip(
        columns,
        1,
        1,
        lambda s: jnp.concatenate([oth2a[s], oth2b[s]], 0),
        lambda s: jnp.concatenate([oth3a[s], oth3b[s]], 0),
    )

    def finish(missing):
        for n, (s, halves) in enumerate(zip(late_halves(), missing, strict=True)):
            acc = partial[n]
            for h in halves:
                acc += dot(row[:, lanes(h, half)], columns[s, lanes(h, half)])
            square[:, lanes(s, half)] = acc.astype(square.dtype)

    @pl.when(home() == 1)
    def _():
        below = (5 - y, 7 - y)
        finish((below, below, (7 - y,), (4, 5, 7 - y)))

    @pl.when(home() == 0)
    def _():
        below = (3 - y, 5 - y, 7 - y)
        finish((below, below, (2, 3), (2, 3)))

    s = 2 * ((2 * x + y) ^ z) + c
    out[...] = 3.0 * square[:, lanes(s, half)].astype(jnp.float32) - 2.0 * dot(square[...], columns[s])


def call(kernel, name, flops, args, outs, aliases=None, where=pltpu.VMEM, scratch=()):
    return pl.pallas_call(
        kernel,
        out_shape=outs,
        in_specs=[pl.BlockSpec(memory_space=where)] * len(args),
        out_specs=[pl.BlockSpec(memory_space=pltpu.VMEM)] * len(outs),
        scratch_shapes=scratch,
        input_output_aliases=aliases or {},
        compiler_params=pltpu.CompilerParams(vmem_limit_bytes=16 * MIB),
        cost_estimate=pl.CostEstimate(flops=flops, bytes_accessed=0, transcendentals=0),
        name=name,
    )(*args)


def after(value, *others):
    return lax.optimization_barrier((value, *others))[0]


def gathered(density):
    blk, half = density.shape[0], density.shape[0] // 2
    z, x, d, y, c = place()
    cube = blk**3

    def by_z(v, m):
        return lax.ppermute(v, "row", [(i, i ^ m) for i in range(lax.axis_size("row"))])

    def by_x(v):
        return lax.ppermute(v, "col", [(i, i ^ 1) for i in range(lax.axis_size("col"))])

    def by_depth(v, m):
        return lax.ppermute(v, "depth", [(i, i ^ m) for i in range(lax.axis_size("depth"))])

    def quarter(array, k):
        return lax.dynamic_slice(array, (y * half, k * blk + c * half), (half, half))

    def shape(*dims, dtype=jnp.bfloat16):
        return jax.ShapeDtypeStruct(dims, dtype)

    row_shape = shape(blk, 4 * blk)
    columns_shape = shape(8, 4 * blk, half)
    pick = picked(z, x)
    sent = quarter(density, pick)
    two_away = by_z(sent, 2)
    half_row, third = call(
        slices_kernel,
        "slices",
        40 * cube,
        (density, sent),
        (shape(half, 2 * blk), shape(half, half)),
        where=pl.ANY,
        scratch=[pltpu.SemaphoreType.DMA((2,))],
    )
    near = by_x(half_row)
    three_away = by_z(third, 3)
    one_away = by_z(jnp.where(lax.div(z, 2) == x, sent, two_away), 1)
    far = by_depth(near, 1)
    own0 = jnp.stack([two_away, one_away, three_away])
    oth0, own2 = by_x(own0), by_depth(own0, 2)
    own1 = by_depth(own0, 1)
    row, columns, square = call(
        row_kernel,
        "row_blocks",
        18 * cube,
        (own0, own1, near, far, density),
        (row_shape, columns_shape, row_shape),
    )
    oth2a = by_depth(oth0[:, : half // 2], 2)
    oth2b = by_x(own2[:, half // 2 :])
    own3, oth1 = by_depth(own2, 1), by_depth(oth0, 1)
    columns, square, partial = call(
        middle_kernel,
        "middle_blocks",
        30 * cube,
        (row, columns, square, own2, own3, oth0, oth1),
        (columns_shape, row_shape, shape(4, blk, half, dtype=jnp.float32)),
        {1: 0, 2: 1},
    )
    oth2a, oth2b, partial = lax.optimization_barrier((oth2a, oth2b, partial))
    oth3a, oth3b = by_depth(oth2a, 1), by_depth(oth2b, 1)
    return call(
        last_kernel,
        "last_blocks",
        10 * cube,
        (row, columns, square, partial, oth2a, oth2b, oth3a, oth3b),
        (shape(blk, half, dtype=jnp.float32), columns_shape, row_shape),
        {1: 1, 2: 2},
    )[0]


def solution(mesh):
    four_by_two = mesh.shape["row"] == mesh.shape["depth"] == 2 * mesh.shape["col"] == 4
    return jax.shard_map(
        gathered if four_by_two else split_products,
        mesh=mesh,
        in_specs=(P("row", "col"),),
        out_specs=P("row", ("col", "depth")),
        check_vma=False,
    )
```

```python
import functools

import jax
import jax.numpy as jnp
from jax import lax
from jax.experimental import pallas as pl
from jax.experimental.pallas import tpu as pltpu
from jax.sharding import PartitionSpec as P

MIB = 1024 * 1024


def split_products(density):
    rows_blk, cols_blk = density.shape
    depth_n = lax.axis_size("depth")
    strip_len = rows_blk // depth_n
    groups = cols_blk // rows_blk
    layer_idx = lax.axis_index("depth")
    col_strips = lax.dynamic_index_in_dim(
        density.reshape(rows_blk, groups, depth_n, strip_len), layer_idx, 2, keepdims=False
    ).reshape(rows_blk, groups * strip_len)
    row_strips = lax.dynamic_index_in_dim(
        density.reshape(depth_n, strip_len, cols_blk), layer_idx, 0, keepdims=False
    )

    def gather_slab(local_slab):
        return lax.all_gather(local_slab, "col", axis=1, tiled=True)

    def multiply(left_full):
        return jnp.dot(
            left_full,
            lax.all_gather(row_strips, "row", axis=0, tiled=True),
            preferred_element_type=jnp.float32,
        )

    partial_square = multiply(gather_slab(col_strips))
    square = lax.psum(partial_square, "depth").astype(jnp.bfloat16)
    square_strips = lax.dynamic_index_in_dim(
        square.reshape(rows_blk, groups, depth_n, strip_len), layer_idx, 2, keepdims=False
    ).reshape(rows_blk, groups * strip_len)
    partial_cube = multiply(gather_slab(square_strips))
    cube_sum = lax.psum_scatter(-2.0 * partial_cube, "depth", scatter_dimension=1, tiled=True)
    share_width = cols_blk // depth_n
    own_square = lax.dynamic_slice_in_dim(square, layer_idx * share_width, share_width, 1).astype(
        jnp.float32
    )
    return cube_sum + 3.0 * own_square


def dot(a, b):
    return jnp.dot(a, b, preferred_element_type=jnp.float32)


def dot_t(a, b):
    return lax.dot_general(a, b, (((1,), (1,)), ((), ())), preferred_element_type=jnp.float32)


def turned(a):
    return jnp.transpose(a)


def place():
    z, x, d = lax.axis_index("row"), lax.axis_index("col"), lax.axis_index("depth")
    return z, x, d, lax.div(d, 2), lax.rem(d, 2)


def picked(z, x):
    return lax.rem(z, 2) ^ lax.div(z, 2) ^ x


def received(slot, other):
    z, x, _, _, _ = place()
    away = x ^ other ^ lax.div(z, 2)
    if slot == 0:
        return 2, 1 + away
    if slot == 1:
        return 1 + 2 * away, 1 + 2 * away
    return 3, 1 + away


def lanes(s, half):
    return pl.ds(pl.multiple_of(s * half, half), half)


def put(columns, i, k, quarter):
    half = quarter.shape[0]
    columns[k, lanes(i, half)] = quarter
    columns[i, lanes(k, half)] = turned(quarter)


def put_strip(columns, other, y_dist, same_core, other_core):
    _, _, _, y, c = place()
    for slot in range(3):
        i, k = received(slot, other)
        for cc, quarter in ((c, same_core(slot)), (1 - c, other_core(slot))):
            put(columns, 2 * i + (y ^ y_dist), 2 * k + cc, quarter)


def put_row(row, columns, m, rows, piece):
    half = columns.shape[2]
    for h in range(2):
        part = piece[:, h * half : (h + 1) * half]
        row[lanes(rows, half), lanes(2 * m + h, half)] = part
        put(columns, rows, 2 * m + h, part)


def home():
    z, x, _, _, _ = place()
    return (x == lax.div(z, 2)).astype(jnp.int32)


def early_halves():
    _, _, _, y, _ = place()
    at_home = home()
    return 0, 1, (4 + y) * (1 - at_home) + 2 * at_home, (6 + y) * (1 - at_home) + 3 * at_home


def late_halves():
    _, _, _, y, _ = place()
    at_home = home()
    return (
        2 + 2 * at_home,
        3 + 2 * at_home,
        (5 - y) * (1 - at_home) + (6 + y) * at_home,
        (7 - y),
    )


def half_kernel(array, before, out, upper):
    del before
    out[...] = array[:, : out.shape[1]] if upper else array[:, out.shape[1] :]


def join_kernel(a, b, before, out):
    del before
    out[: a.shape[0]] = a[...]
    out[a.shape[0] :] = b[...]


def stack_kernel(a, b, c, before, out):
    del before
    for n, ref in enumerate((a, b, c)):
        out[n] = ref[...]


def fetch(source, out, sem):
    copy = pltpu.make_async_copy(source, out, sem)
    copy.start()
    copy.wait()


def half_row_kernel(density, before, out, sem):
    del before
    _, _, _, _, c = place()
    fetch(density.at[lanes(c, out.shape[0])], out, sem)


def third_kernel(density, before, out, sem):
    del before
    z, x, _, y, c = place()
    half = out.shape[0]
    fetch(density.at[lanes(y, half), lanes(2 * (1 - picked(z, x)) + c, half)], out, sem)


def own_kernel(own, own_turned, own_square):
    half = own_turned.shape[2]
    for h in range(2):
        rows = own[h * half : (h + 1) * half, :]
        own_square[h] = dot_t(own[...], rows)
        for s in range(4):
            own_turned[h, s * half : (s + 1) * half] = turned(rows[:, s * half : (s + 1) * half])


def middle_kernel(
    own, own_turned, own_square, near, far, own0, own1, own2, own3, oth0, oth1, row, columns, square, partial
):
    z, x, _, y, c = place()
    blk, half = near.shape[1] // 2, columns.shape[2]
    for b in range(2):
        m = (2 * x + b) ^ z
        for h in range(2):
            part = own[:, (2 * b + h) * half : (2 * b + h + 1) * half]
            row[:, lanes(2 * m + h, half)] = part
            columns[2 * m + h, :blk] = part
            columns[h, pl.ds(pl.multiple_of(m * blk, blk), blk)] = own_turned[h, b * blk : (b + 1) * blk]
        m = (2 * (1 - x) + b) ^ z
        put_row(row, columns, m, c, near[:, b * blk : (b + 1) * blk])
        put_row(row, columns, m, 1 - c, far[:, b * blk : (b + 1) * blk])
    put_strip(columns, 0, 0, lambda s: own0[s], lambda s: own1[s])
    put_strip(columns, 0, 1, lambda s: own2[s], lambda s: own3[s])
    put_strip(columns, 1, 0, lambda s: oth0[s], lambda s: oth1[s])
    nothing = jnp.zeros((half, half), columns.dtype)
    for slot in range(3):
        i, k = received(slot, 1)
        for h in range(2):
            columns[2 * k + h, lanes(2 * i + 1 - y, half)] = nothing

            @pl.when(i != k)
            def _(i=i, k=k, h=h):
                columns[2 * i + 1 - y, lanes(2 * k + h, half)] = nothing

    others = pl.ds(pl.multiple_of(2 * blk * home(), 2 * blk), 2 * blk)
    for h in range(2):
        acc = own_square[h] + dot(row[:, others], columns[h, others])
        square[:, h * half : (h + 1) * half] = acc.astype(square.dtype)
    for s in early_halves()[2:]:
        square[:, lanes(s, half)] = dot(row[...], columns[s]).astype(square.dtype)
    for n, s in enumerate(late_halves()):
        partial[n] = dot(row[...], columns[s])


def add_last(row, columns, partial, upper, lower, cc):
    _, _, _, y, _ = place()
    half = columns.shape[2]
    quarters = [jnp.concatenate([upper[slot], lower[slot]], 0) for slot in range(3)]
    for slot, q in enumerate(quarters):
        i, k = received(slot, 1)
        put(columns, 2 * i + 1 - y, 2 * k + cc, q)
    two, one, three = quarters

    def rows(s):
        return row[:, lanes(s, half)]

    @pl.when(home() == 1)
    def _():
        partial[cc] += dot(rows(5 - y), two) + dot(rows(7 - y), three)
        partial[3 - (cc ^ y ^ 1)] += dot(rows(7 - y), one)
        partial[3] += dot_t(rows(4 + cc), three)

    @pl.when(home() == 0)
    def _():
        partial[cc] += dot(rows(5 - y), two) + dot(rows(3 - y), one) + dot(rows(7 - y), three)
        partial[2] += dot_t(rows(2 + cc), two)
        partial[3] += dot_t(rows(2 + cc), three)


def finish_kernel(row, columns_in, partial_in, oth2a, oth2b, columns, partial):
    del columns_in, partial_in
    add_last(row, columns, partial, oth2a, oth2b, place()[4])


def last_kernel(row, columns_in, square_in, partial_in, oth3a, oth3b, out, columns, square, partial):
    del columns_in, square_in, partial_in
    z, x, _, y, c = place()
    half = columns.shape[2]
    add_last(row, columns, partial, oth3a, oth3b, 1 - c)
    for n, s in enumerate(late_halves()):
        square[:, lanes(s, half)] = partial[n].astype(square.dtype)
    s = 2 * ((2 * x + y) ^ z) + c
    out[...] = 3.0 * square[:, lanes(s, half)].astype(jnp.float32) - 2.0 * dot(square[...], columns[s])


def call(kernel, name, flops, args, outs, aliases=None, order_only=0, scratch=()):
    return pl.pallas_call(
        kernel,
        out_shape=outs,
        in_specs=[pl.BlockSpec(memory_space=pltpu.VMEM)] * (len(args) - order_only)
        + [pl.BlockSpec(memory_space=pl.ANY)] * order_only,
        out_specs=[pl.BlockSpec(memory_space=pltpu.VMEM)] * len(outs),
        scratch_shapes=scratch,
        input_output_aliases=aliases or {},
        compiler_params=pltpu.CompilerParams(vmem_limit_bytes=16 * MIB),
        cost_estimate=pl.CostEstimate(flops=flops, bytes_accessed=0, transcendentals=0),
        name=name,
    )(*args)


def after(value, *others):
    return lax.optimization_barrier((value, *others))[0]


def gathered(density):
    blk, half = density.shape[0], density.shape[0] // 2
    z, x, d, y, c = place()
    cube = blk**3

    def by_z(v, m):
        return lax.ppermute(v, "row", [(i, i ^ m) for i in range(lax.axis_size("row"))])

    def by_x(v):
        return lax.ppermute(v, "col", [(i, i ^ 1) for i in range(lax.axis_size("col"))])

    def by_depth(v, m):
        return lax.ppermute(v, "depth", [(i, i ^ m) for i in range(lax.axis_size("depth"))])

    def quarter(array, k):
        return lax.dynamic_slice(array, (y * half, k * blk + c * half), (half, half))

    def shape(*dims, dtype=jnp.bfloat16):
        return jax.ShapeDtypeStruct(dims, dtype)

    row_shape = shape(blk, 4 * blk)
    columns_shape = shape(8, 4 * blk, half)
    pick = picked(z, x)
    sent = quarter(density, pick)
    two_away = by_z(sent, 2)
    half_row = call(
        half_row_kernel,
        "half_row",
        40 * cube,
        (density, sent),
        (shape(half, 2 * blk),),
        order_only=2,
        scratch=[pltpu.SemaphoreType.DMA],
    )[0]
    third = call(
        third_kernel,
        "third",
        20 * cube,
        (density, half_row),
        (shape(half, half),),
        order_only=2,
        scratch=[pltpu.SemaphoreType.DMA],
    )[0]
    near = by_x(half_row)
    three_away = by_z(third, 3)
    one_away = by_z(jnp.where(lax.div(z, 2) == x, sent, two_away), 1)
    far = by_depth(near, 1)
    own_turned, own_square = call(
        own_kernel,
        "own_blocks",
        8 * cube,
        (density,),
        (shape(2, 2 * blk, half), shape(2, blk, half, dtype=jnp.float32)),
    )
    own0 = call(
        stack_kernel,
        "stack",
        0,
        (two_away, one_away, three_away, own_turned),
        (shape(3, half, half),),
        order_only=1,
    )[0]
    oth0, own2 = by_x(own0), by_depth(own0, 2)
    own1 = by_depth(own0, 1)
    oth2a = by_depth(oth0[:, : half // 2], 2)
    oth2b = by_x(own2[:, half // 2 :])
    own3, oth1 = by_depth(own2, 1), by_depth(oth0, 1)
    row, columns, square, partial = call(
        middle_kernel,
        "middle_blocks",
        30 * cube,
        (density, own_turned, own_square, near, far, own0, own1, own2, own3, oth0, oth1),
        (row_shape, columns_shape, row_shape, shape(4, blk, half, dtype=jnp.float32)),
    )
    oth2a, oth2b, partial = lax.optimization_barrier((oth2a, oth2b, partial))
    oth3a, oth3b = by_depth(oth2a, 1), by_depth(oth2b, 1)
    partial_shape = shape(4, blk, half, dtype=jnp.float32)
    columns, partial = call(
        finish_kernel,
        "finish_blocks",
        4 * cube,
        (row, columns, partial, oth2a, oth2b),
        (columns_shape, partial_shape),
        {1: 0, 2: 1},
    )
    return call(
        last_kernel,
        "last_blocks",
        8 * cube,
        (row, columns, square, partial, oth3a, oth3b),
        (shape(blk, half, dtype=jnp.float32), columns_shape, row_shape, partial_shape),
        {1: 1, 2: 2, 3: 3},
    )[0]


def solution(mesh):
    four_by_two = mesh.shape["row"] == mesh.shape["depth"] == 2 * mesh.shape["col"] == 4
    return jax.shard_map(
        gathered if four_by_two else split_products,
        mesh=mesh,
        in_specs=(P("row", "col"),),
        out_specs=P("row", ("col", "depth")),
        check_vma=False,
    )
```

```python
import functools

import jax
import jax.numpy as jnp
from jax import lax
from jax.experimental import pallas as pl
from jax.experimental.pallas import tpu as pltpu
from jax.sharding import PartitionSpec as P

MIB = 1024 * 1024


def split_products(density):
    rows_blk, cols_blk = density.shape
    depth_n = lax.axis_size("depth")
    strip_len = rows_blk // depth_n
    groups = cols_blk // rows_blk
    layer_idx = lax.axis_index("depth")
    col_strips = lax.dynamic_index_in_dim(
        density.reshape(rows_blk, groups, depth_n, strip_len), layer_idx, 2, keepdims=False
    ).reshape(rows_blk, groups * strip_len)
    row_strips = lax.dynamic_index_in_dim(
        density.reshape(depth_n, strip_len, cols_blk), layer_idx, 0, keepdims=False
    )

    def gather_slab(local_slab):
        return lax.all_gather(local_slab, "col", axis=1, tiled=True)

    def multiply(left_full):
        return jnp.dot(
            left_full,
            lax.all_gather(row_strips, "row", axis=0, tiled=True),
            preferred_element_type=jnp.float32,
        )

    partial_square = multiply(gather_slab(col_strips))
    square = lax.psum(partial_square, "depth").astype(jnp.bfloat16)
    square_strips = lax.dynamic_index_in_dim(
        square.reshape(rows_blk, groups, depth_n, strip_len), layer_idx, 2, keepdims=False
    ).reshape(rows_blk, groups * strip_len)
    partial_cube = multiply(gather_slab(square_strips))
    cube_sum = lax.psum_scatter(-2.0 * partial_cube, "depth", scatter_dimension=1, tiled=True)
    share_width = cols_blk // depth_n
    own_square = lax.dynamic_slice_in_dim(square, layer_idx * share_width, share_width, 1).astype(
        jnp.float32
    )
    return cube_sum + 3.0 * own_square


def dot(a, b):
    return jnp.dot(a, b, preferred_element_type=jnp.float32)


def dot_t(a, b):
    return lax.dot_general(a, b, (((1,), (1,)), ((), ())), preferred_element_type=jnp.float32)


def turned(a):
    return jnp.transpose(a)


def place():
    z, x, d = lax.axis_index("row"), lax.axis_index("col"), lax.axis_index("depth")
    return z, x, d, lax.div(d, 2), lax.rem(d, 2)


def picked(z, x):
    return lax.rem(z, 2) ^ lax.div(z, 2) ^ x


def received(slot, other):
    z, x, _, _, _ = place()
    away = x ^ other ^ lax.div(z, 2)
    if slot == 0:
        return 2, 1 + away
    if slot == 1:
        return 1 + 2 * away, 1 + 2 * away
    return 3, 1 + away


def lanes(s, half):
    return pl.ds(pl.multiple_of(s * half, half), half)


def put(columns, i, k, quarter):
    half = quarter.shape[0]
    columns[k, lanes(i, half)] = quarter
    columns[i, lanes(k, half)] = turned(quarter)


def put_strip(columns, other, y_dist, same_core, other_core):
    _, _, _, y, c = place()
    for slot in range(3):
        i, k = received(slot, other)
        for cc, quarter in ((c, same_core(slot)), (1 - c, other_core(slot))):
            put(columns, 2 * i + (y ^ y_dist), 2 * k + cc, quarter)


def put_row(row, columns, m, rows, piece):
    half = columns.shape[2]
    for h in range(2):
        part = piece[:, h * half : (h + 1) * half]
        row[lanes(rows, half), lanes(2 * m + h, half)] = part
        put(columns, rows, 2 * m + h, part)


def home():
    z, x, _, _, _ = place()
    return (x == lax.div(z, 2)).astype(jnp.int32)


def early_halves():
    _, _, _, y, _ = place()
    at_home = home()
    return 0, 1, (4 + y) * (1 - at_home) + 2 * at_home, (6 + y) * (1 - at_home) + 3 * at_home


def late_halves():
    _, _, _, y, _ = place()
    at_home = home()
    return (
        2 + 2 * at_home,
        3 + 2 * at_home,
        (5 - y) * (1 - at_home) + (6 + y) * at_home,
        (7 - y),
    )


def half_kernel(array, before, out, upper):
    del before
    out[...] = array[:, : out.shape[1]] if upper else array[:, out.shape[1] :]


def join_kernel(a, b, before, out):
    del before
    out[: a.shape[0]] = a[...]
    out[a.shape[0] :] = b[...]


def stack_kernel(a, b, c, out):
    for n, ref in enumerate((a, b, c)):
        out[n] = ref[...]


def fetch(source, out, sem):
    copy = pltpu.make_async_copy(source, out, sem)
    copy.start()
    copy.wait()


def half_row_kernel(density, before, out, sem):
    del before
    _, _, _, _, c = place()
    fetch(density.at[lanes(c, out.shape[0])], out, sem)


def third_kernel(density, before, out, sem):
    del before
    z, x, _, y, c = place()
    half = out.shape[0]
    fetch(density.at[lanes(y, half), lanes(2 * (1 - picked(z, x)) + c, half)], out, sem)


def first_kernel(own, own0, own1, row, columns):
    z, x, _, _, _ = place()
    blk, half = own.shape[0], columns.shape[2]
    for b in range(2):
        m = (2 * x + b) ^ z
        for h in range(2):
            part = own[:, (2 * b + h) * half : (2 * b + h + 1) * half]
            row[:, lanes(2 * m + h, half)] = part
            columns[2 * m + h, :blk] = part
            for g in range(2):
                columns[g, lanes(2 * m + h, half)] = turned(part[g * half : (g + 1) * half])
    put_strip(columns, 0, 0, lambda s: own0[s], lambda s: own1[s])


def cross_kernel(a, b, before, out):
    del before
    _, _, _, _, c = place()

    @pl.when(c == 0)
    def _():
        out[...] = a[...]

    @pl.when(c == 1)
    def _():
        out[...] = b[...]


def middle_kernel(row_in, columns_in, near, far, own2, own3, oth0, oth1, row, columns, square, partial):
    del row_in, columns_in
    z, x, _, y, c = place()
    blk, half = near.shape[1] // 2, columns.shape[2]
    for b in range(2):
        m = (2 * (1 - x) + b) ^ z
        put_row(row, columns, m, c, near[:, b * blk : (b + 1) * blk])
        put_row(row, columns, m, 1 - c, far[:, b * blk : (b + 1) * blk])
    put_strip(columns, 0, 1, lambda s: own2[s], lambda s: own3[s])
    put_strip(columns, 1, 0, lambda s: oth0[s], lambda s: oth1[s])
    nothing = jnp.zeros((half, half), columns.dtype)
    for slot in range(3):
        i, k = received(slot, 1)
        for h in range(2):
            columns[2 * k + h, lanes(2 * i + 1 - y, half)] = nothing

            @pl.when(i != k)
            def _(i=i, k=k, h=h):
                columns[2 * i + 1 - y, lanes(2 * k + h, half)] = nothing

    for s in early_halves():
        square[:, lanes(s, half)] = dot(row[...], columns[s]).astype(square.dtype)
    for n, s in enumerate(late_halves()):
        partial[n] = dot(row[...], columns[s])


def add_last(row, columns, partial, last, cc):
    _, _, _, y, _ = place()
    half = columns.shape[2]
    quarters = [last[slot] for slot in range(3)]
    for slot, q in enumerate(quarters):
        i, k = received(slot, 1)
        put(columns, 2 * i + 1 - y, 2 * k + cc, q)
    two, one, three = quarters

    def rows(s):
        return row[:, lanes(s, half)]

    @pl.when(home() == 1)
    def _():
        partial[cc] += dot(rows(5 - y), two) + dot(rows(7 - y), three)
        partial[3 - (cc ^ y ^ 1)] += dot(rows(7 - y), one)
        partial[3] += dot_t(rows(4 + cc), three)

    @pl.when(home() == 0)
    def _():
        partial[cc] += dot(rows(5 - y), two) + dot(rows(3 - y), one) + dot(rows(7 - y), three)
        partial[2] += dot_t(rows(2 + cc), two)
        partial[3] += dot_t(rows(2 + cc), three)


def wanted():
    z, x, _, y, c = place()
    return 2 * ((2 * x + y) ^ z) + c


def finish_kernel(row, columns_in, partial_in, square, oth2, columns, partial, cube):
    del columns_in, partial_in
    half = columns.shape[2]
    add_last(row, columns, partial, oth2, place()[4])
    s = wanted()
    acc = None
    for h in early_halves():
        term = dot(square[:, lanes(h, half)], columns[s, lanes(h, half)])
        acc = term if acc is None else acc + term
    cube[...] = acc


def last_kernel(row, columns_in, square_in, partial_in, cube, oth3, out, columns, square, partial):
    del columns_in, square_in, partial_in
    half = columns.shape[2]
    add_last(row, columns, partial, oth3, 1 - place()[4])
    s = wanted()
    acc = cube[...]
    for n, h in enumerate(late_halves()):
        part = partial[n].astype(square.dtype)
        square[:, lanes(h, half)] = part
        acc += dot(part, columns[s, lanes(h, half)])
    out[...] = 3.0 * square[:, lanes(s, half)].astype(jnp.float32) - 2.0 * acc


def call(kernel, name, flops, args, outs, aliases=None, order_only=0, scratch=()):
    return pl.pallas_call(
        kernel,
        out_shape=outs,
        in_specs=[pl.BlockSpec(memory_space=pltpu.VMEM)] * (len(args) - order_only)
        + [pl.BlockSpec(memory_space=pl.ANY)] * order_only,
        out_specs=[pl.BlockSpec(memory_space=pltpu.VMEM)] * len(outs),
        scratch_shapes=scratch,
        input_output_aliases=aliases or {},
        compiler_params=pltpu.CompilerParams(vmem_limit_bytes=16 * MIB),
        cost_estimate=pl.CostEstimate(flops=flops, bytes_accessed=0, transcendentals=0),
        name=name,
    )(*args)


def after(value, *others):
    return lax.optimization_barrier((value, *others))[0]


def gathered(density):
    blk, half = density.shape[0], density.shape[0] // 2
    z, x, d, y, c = place()
    cube = blk**3

    def by_z(v, m):
        return lax.ppermute(v, "row", [(i, i ^ m) for i in range(lax.axis_size("row"))])

    def by_x(v):
        return lax.ppermute(v, "col", [(i, i ^ 1) for i in range(lax.axis_size("col"))])

    def by_depth(v, m):
        return lax.ppermute(v, "depth", [(i, i ^ m) for i in range(lax.axis_size("depth"))])

    def crossed(v):
        n = lax.axis_size("depth")
        pairs = [(p, p ^ 2 if p % 2 == 0 else p ^ n) for p in range(lax.axis_size("col") * n)]
        return lax.ppermute(v, ("col", "depth"), pairs)

    def quarter(array, k):
        return lax.dynamic_slice(array, (y * half, k * blk + c * half), (half, half))

    def shape(*dims, dtype=jnp.bfloat16):
        return jax.ShapeDtypeStruct(dims, dtype)

    row_shape = shape(blk, 4 * blk)
    columns_shape = shape(8, 4 * blk, half)
    pick = picked(z, x)
    sent = quarter(density, pick)
    two_away = by_z(sent, 2)
    half_row = call(
        half_row_kernel,
        "half_row",
        40 * cube,
        (density, sent),
        (shape(half, 2 * blk),),
        order_only=2,
        scratch=[pltpu.SemaphoreType.DMA],
    )[0]
    third = call(
        third_kernel,
        "third",
        20 * cube,
        (density, half_row),
        (shape(half, half),),
        order_only=2,
        scratch=[pltpu.SemaphoreType.DMA],
    )[0]
    near = by_x(half_row)
    three_away = by_z(third, 3)
    one_away = by_z(jnp.where(lax.div(z, 2) == x, sent, two_away), 1)
    far = by_depth(near, 1)
    own0 = call(
        stack_kernel,
        "stack",
        0,
        (two_away, one_away, three_away),
        (shape(3, half, half),),
    )[0]
    oth0, own2 = by_x(own0), by_depth(own0, 2)
    own1 = by_depth(own0, 1)
    row, columns = call(
        first_kernel, "first_blocks", 2 * cube, (density, own0, own1), (row_shape, columns_shape)
    )
    diagonal = call(
        cross_kernel, "cross", 0, (oth0, own2, row), (shape(3, half, half),), order_only=1
    )[0]
    oth2 = crossed(diagonal)
    own3, oth1 = by_depth(own2, 1), by_depth(oth0, 1)
    row, columns, square, partial = call(
        middle_kernel,
        "middle_blocks",
        30 * cube,
        (row, columns, near, far, own2, own3, oth0, oth1),
        (row_shape, columns_shape, row_shape, shape(4, blk, half, dtype=jnp.float32)),
        {0: 0, 1: 1},
    )
    oth2, partial = lax.optimization_barrier((oth2, partial))
    oth3 = by_depth(oth2, 1)
    partial_shape = shape(4, blk, half, dtype=jnp.float32)
    out_shape = shape(blk, half, dtype=jnp.float32)
    columns, partial, early = call(
        finish_kernel,
        "finish_blocks",
        4 * cube,
        (row, columns, partial, square, oth2),
        (columns_shape, partial_shape, out_shape),
        {1: 0, 2: 1},
    )
    return call(
        last_kernel,
        "last_blocks",
        8 * cube,
        (row, columns, square, partial, early, oth3),
        (out_shape, columns_shape, row_shape, partial_shape),
        {1: 1, 2: 2, 3: 3},
    )[0]


def solution(mesh):
    four_by_two = mesh.shape["row"] == mesh.shape["depth"] == 2 * mesh.shape["col"] == 4
    return jax.shard_map(
        gathered if four_by_two else split_products,
        mesh=mesh,
        in_specs=(P("row", "col"),),
        out_specs=P("row", ("col", "depth")),
        check_vma=False,
    )
```

```python
import functools

import jax
import jax.numpy as jnp
from jax import lax
from jax.experimental import pallas as pl
from jax.experimental.pallas import tpu as pltpu
from jax.sharding import PartitionSpec as P

MIB = 1024 * 1024


def split_products(density):
    rows_blk, cols_blk = density.shape
    depth_n = lax.axis_size("depth")
    strip_len = rows_blk // depth_n
    groups = cols_blk // rows_blk
    layer_idx = lax.axis_index("depth")
    col_strips = lax.dynamic_index_in_dim(
        density.reshape(rows_blk, groups, depth_n, strip_len), layer_idx, 2, keepdims=False
    ).reshape(rows_blk, groups * strip_len)
    row_strips = lax.dynamic_index_in_dim(
        density.reshape(depth_n, strip_len, cols_blk), layer_idx, 0, keepdims=False
    )

    def gather_slab(local_slab):
        return lax.all_gather(local_slab, "col", axis=1, tiled=True)

    def multiply(left_full):
        return jnp.dot(
            left_full,
            lax.all_gather(row_strips, "row", axis=0, tiled=True),
            preferred_element_type=jnp.float32,
        )

    partial_square = multiply(gather_slab(col_strips))
    square = lax.psum(partial_square, "depth").astype(jnp.bfloat16)
    square_strips = lax.dynamic_index_in_dim(
        square.reshape(rows_blk, groups, depth_n, strip_len), layer_idx, 2, keepdims=False
    ).reshape(rows_blk, groups * strip_len)
    partial_cube = multiply(gather_slab(square_strips))
    cube_sum = lax.psum_scatter(-2.0 * partial_cube, "depth", scatter_dimension=1, tiled=True)
    share_width = cols_blk // depth_n
    own_square = lax.dynamic_slice_in_dim(square, layer_idx * share_width, share_width, 1).astype(
        jnp.float32
    )
    return cube_sum + 3.0 * own_square


def dot(a, b):
    return jnp.dot(a, b, preferred_element_type=jnp.float32)


def dot_t(a, b):
    return lax.dot_general(a, b, (((1,), (1,)), ((), ())), preferred_element_type=jnp.float32)


def turned(a):
    return jnp.transpose(a)


def place():
    z, x, d = lax.axis_index("row"), lax.axis_index("col"), lax.axis_index("depth")
    return z, x, d, lax.div(d, 2), lax.rem(d, 2)


def picked(z, x):
    return lax.rem(z, 2) ^ lax.div(z, 2) ^ x


def received(slot, other):
    z, x, _, _, _ = place()
    away = x ^ other ^ lax.div(z, 2)
    if slot == 0:
        return 2, 1 + away
    if slot == 1:
        return 1 + 2 * away, 1 + 2 * away
    return 3, 1 + away


def lanes(s, half):
    return pl.ds(pl.multiple_of(s * half, half), half)


def put(columns, i, k, quarter):
    half = quarter.shape[0]
    columns[k, lanes(i, half)] = quarter
    columns[i, lanes(k, half)] = turned(quarter)


def put_strip(columns, other, y_dist, same_core, other_core):
    _, _, _, y, c = place()
    for slot in range(3):
        i, k = received(slot, other)
        for cc, quarter in ((c, same_core(slot)), (1 - c, other_core(slot))):
            put(columns, 2 * i + (y ^ y_dist), 2 * k + cc, quarter)


def put_row(row, columns, m, rows, piece):
    half = columns.shape[2]
    for h in range(2):
        part = piece[:, h * half : (h + 1) * half]
        row[lanes(rows, half), lanes(2 * m + h, half)] = part
        put(columns, rows, 2 * m + h, part)


def home():
    z, x, _, _, _ = place()
    return (x == lax.div(z, 2)).astype(jnp.int32)


def early_halves():
    _, _, _, y, _ = place()
    at_home = home()
    return 0, 1, (4 + y) * (1 - at_home) + 2 * at_home, (6 + y) * (1 - at_home) + 3 * at_home


def late_halves():
    _, _, _, y, _ = place()
    at_home = home()
    return (
        2 + 2 * at_home,
        3 + 2 * at_home,
        (5 - y) * (1 - at_home) + (6 + y) * at_home,
        (7 - y),
    )


def half_kernel(array, before, out, upper):
    del before
    out[...] = array[:, : out.shape[1]] if upper else array[:, out.shape[1] :]


def join_kernel(a, b, before, out):
    del before
    out[: a.shape[0]] = a[...]
    out[a.shape[0] :] = b[...]


def stack_kernel(a, b, c, out):
    for n, ref in enumerate((a, b, c)):
        out[n] = ref[...]


def fetch(source, out, sem):
    copy = pltpu.make_async_copy(source, out, sem)
    copy.start()
    copy.wait()


def half_row_kernel(density, before, out, sem):
    del before
    _, _, _, _, c = place()
    fetch(density.at[lanes(c, out.shape[0])], out, sem)


def third_kernel(density, before, out, sem):
    del before
    z, x, _, y, c = place()
    half = out.shape[0]
    fetch(density.at[lanes(y, half), lanes(2 * (1 - picked(z, x)) + c, half)], out, sem)


def first_kernel(own, own0, row, columns):
    z, x, _, y, c = place()
    blk, half = own.shape[0], columns.shape[2]
    for b in range(2):
        m = (2 * x + b) ^ z
        for h in range(2):
            part = own[:, (2 * b + h) * half : (2 * b + h + 1) * half]
            row[:, lanes(2 * m + h, half)] = part
            columns[2 * m + h, :blk] = part
            for g in range(2):
                columns[g, lanes(2 * m + h, half)] = turned(part[g * half : (g + 1) * half])
    for slot in range(3):
        i, k = received(slot, 0)
        put(columns, 2 * i + y, 2 * k + c, own0[slot])


def pass_kernel(a, before, out):
    del before
    out[...] = a[...]


def cross_kernel(a, b, before, out):
    del before
    _, _, _, _, c = place()

    @pl.when(c == 0)
    def _():
        out[...] = a[...]

    @pl.when(c == 1)
    def _():
        out[...] = b[...]


def middle_kernel(row_in, columns_in, near, far, own1, own2, own3, oth0, oth1, row, columns, square, partial):
    del row_in, columns_in
    z, x, _, y, c = place()
    blk, half = near.shape[1] // 2, columns.shape[2]
    for b in range(2):
        m = (2 * (1 - x) + b) ^ z
        put_row(row, columns, m, c, near[:, b * blk : (b + 1) * blk])
        put_row(row, columns, m, 1 - c, far[:, b * blk : (b + 1) * blk])
    for slot in range(3):
        i, k = received(slot, 0)
        put(columns, 2 * i + y, 2 * k + 1 - c, own1[slot])
    put_strip(columns, 0, 1, lambda s: own2[s], lambda s: own3[s])
    put_strip(columns, 1, 0, lambda s: oth0[s], lambda s: oth1[s])
    nothing = jnp.zeros((half, half), columns.dtype)
    for slot in range(3):
        i, k = received(slot, 1)
        for h in range(2):
            columns[2 * k + h, lanes(2 * i + 1 - y, half)] = nothing

            @pl.when(i != k)
            def _(i=i, k=k, h=h):
                columns[2 * i + 1 - y, lanes(2 * k + h, half)] = nothing

    for s in early_halves():
        square[:, lanes(s, half)] = dot(row[...], columns[s]).astype(square.dtype)
    for n, s in enumerate(late_halves()):
        partial[n] = dot(row[...], columns[s])


def add_last(row, columns, partial, last, cc):
    _, _, _, y, _ = place()
    half = columns.shape[2]
    quarters = [last[slot] for slot in range(3)]
    for slot, q in enumerate(quarters):
        i, k = received(slot, 1)
        put(columns, 2 * i + 1 - y, 2 * k + cc, q)
    two, one, three = quarters

    def rows(s):
        return row[:, lanes(s, half)]

    @pl.when(home() == 1)
    def _():
        partial[cc] += dot(rows(5 - y), two) + dot(rows(7 - y), three)
        partial[3 - (cc ^ y ^ 1)] += dot(rows(7 - y), one)
        partial[3] += dot_t(rows(4 + cc), three)

    @pl.when(home() == 0)
    def _():
        partial[cc] += dot(rows(5 - y), two) + dot(rows(3 - y), one) + dot(rows(7 - y), three)
        partial[2] += dot_t(rows(2 + cc), two)
        partial[3] += dot_t(rows(2 + cc), three)


def wanted():
    z, x, _, y, c = place()
    return 2 * ((2 * x + y) ^ z) + c


def finish_kernel(row, columns_in, partial_in, square, oth2, columns, partial, cube):
    del columns_in, partial_in
    half = columns.shape[2]
    add_last(row, columns, partial, oth2, place()[4])
    s = wanted()
    acc = None
    for h in early_halves():
        term = dot(square[:, lanes(h, half)], columns[s, lanes(h, half)])
        acc = term if acc is None else acc + term
    cube[...] = acc


def last_kernel(row, columns_in, square_in, partial_in, cube, oth3, out, columns, square, partial):
    del columns_in, square_in, partial_in
    half = columns.shape[2]
    add_last(row, columns, partial, oth3, 1 - place()[4])
    s = wanted()
    acc = cube[...]
    for n, h in enumerate(late_halves()):
        part = partial[n].astype(square.dtype)
        square[:, lanes(h, half)] = part
        acc += dot(part, columns[s, lanes(h, half)])
    out[...] = 3.0 * square[:, lanes(s, half)].astype(jnp.float32) - 2.0 * acc


def call(kernel, name, flops, args, outs, aliases=None, order_only=0, scratch=()):
    return pl.pallas_call(
        kernel,
        out_shape=outs,
        in_specs=[pl.BlockSpec(memory_space=pltpu.VMEM)] * (len(args) - order_only)
        + [pl.BlockSpec(memory_space=pl.ANY)] * order_only,
        out_specs=[pl.BlockSpec(memory_space=pltpu.VMEM)] * len(outs),
        scratch_shapes=scratch,
        input_output_aliases=aliases or {},
        compiler_params=pltpu.CompilerParams(vmem_limit_bytes=16 * MIB),
        cost_estimate=pl.CostEstimate(flops=flops, bytes_accessed=0, transcendentals=0),
        name=name,
    )(*args)


def after(value, *others):
    return lax.optimization_barrier((value, *others))[0]


def gathered(density):
    blk, half = density.shape[0], density.shape[0] // 2
    z, x, d, y, c = place()
    cube = blk**3

    def by_z(v, m):
        return lax.ppermute(v, "row", [(i, i ^ m) for i in range(lax.axis_size("row"))])

    def by_x(v):
        return lax.ppermute(v, "col", [(i, i ^ 1) for i in range(lax.axis_size("col"))])

    def by_depth(v, m):
        return lax.ppermute(v, "depth", [(i, i ^ m) for i in range(lax.axis_size("depth"))])

    def crossed(v):
        n = lax.axis_size("depth")
        pairs = [(p, p ^ 2 if p % 2 == 0 else p ^ n) for p in range(lax.axis_size("col") * n)]
        return lax.ppermute(v, ("col", "depth"), pairs)

    def quarter(array, k):
        return lax.dynamic_slice(array, (y * half, k * blk + c * half), (half, half))

    def shape(*dims, dtype=jnp.bfloat16):
        return jax.ShapeDtypeStruct(dims, dtype)

    row_shape = shape(blk, 4 * blk)
    columns_shape = shape(8, 4 * blk, half)
    pick = picked(z, x)
    sent = quarter(density, pick)
    two_away = by_z(sent, 2)
    half_row = call(
        half_row_kernel,
        "half_row",
        40 * cube,
        (density, sent),
        (shape(half, 2 * blk),),
        order_only=2,
        scratch=[pltpu.SemaphoreType.DMA],
    )[0]
    third = call(
        third_kernel,
        "third",
        20 * cube,
        (density, half_row),
        (shape(half, half),),
        order_only=2,
        scratch=[pltpu.SemaphoreType.DMA],
    )[0]
    near = by_x(half_row)
    three_away = by_z(third, 3)
    one_away = by_z(jnp.where(lax.div(z, 2) == x, sent, two_away), 1)
    far = by_depth(near, 1)
    own0 = call(
        stack_kernel,
        "stack",
        0,
        (two_away, one_away, three_away),
        (shape(3, half, half),),
    )[0]
    oth0, own2 = by_x(own0), by_depth(own0, 2)
    own1 = by_depth(own0, 1)
    row, columns = call(
        first_kernel, "first_blocks", 2 * cube, (density, own0), (row_shape, columns_shape)
    )
    quarters = shape(3, half, half)
    oth1 = by_depth(call(pass_kernel, "oth0", 0, (oth0, row), (quarters,), order_only=1)[0], 1)
    own3 = by_depth(call(pass_kernel, "own2", 0, (own2, row), (quarters,), order_only=1)[0], 1)
    diagonal = call(
        cross_kernel, "cross", 0, (oth0, own2, row), (shape(3, half, half),), order_only=1
    )[0]
    oth2 = crossed(diagonal)
    row, columns, square, partial = call(
        middle_kernel,
        "middle_blocks",
        30 * cube,
        (row, columns, near, far, own1, own2, own3, oth0, oth1),
        (row_shape, columns_shape, row_shape, shape(4, blk, half, dtype=jnp.float32)),
        {0: 0, 1: 1},
    )
    oth2, partial = lax.optimization_barrier((oth2, partial))
    oth3 = by_depth(oth2, 1)
    partial_shape = shape(4, blk, half, dtype=jnp.float32)
    out_shape = shape(blk, half, dtype=jnp.float32)
    columns, partial, early = call(
        finish_kernel,
        "finish_blocks",
        4 * cube,
        (row, columns, partial, square, oth2),
        (columns_shape, partial_shape, out_shape),
        {1: 0, 2: 1},
    )
    return call(
        last_kernel,
        "last_blocks",
        8 * cube,
        (row, columns, square, partial, early, oth3),
        (out_shape, columns_shape, row_shape, partial_shape),
        {1: 1, 2: 2, 3: 3},
    )[0]


def solution(mesh):
    four_by_two = mesh.shape["row"] == mesh.shape["depth"] == 2 * mesh.shape["col"] == 4
    return jax.shard_map(
        gathered if four_by_two else split_products,
        mesh=mesh,
        in_specs=(P("row", "col"),),
        out_specs=P("row", ("col", "depth")),
        check_vma=False,
    )
```

```python
import functools

import jax
import jax.numpy as jnp
from jax import lax
from jax.experimental import pallas as pl
from jax.experimental.pallas import tpu as pltpu
from jax.sharding import PartitionSpec as P

MIB = 1024 * 1024


def split_products(density):
    rows_blk, cols_blk = density.shape
    depth_n = lax.axis_size("depth")
    strip_len = rows_blk // depth_n
    groups = cols_blk // rows_blk
    layer_idx = lax.axis_index("depth")
    col_strips = lax.dynamic_index_in_dim(
        density.reshape(rows_blk, groups, depth_n, strip_len), layer_idx, 2, keepdims=False
    ).reshape(rows_blk, groups * strip_len)
    row_strips = lax.dynamic_index_in_dim(
        density.reshape(depth_n, strip_len, cols_blk), layer_idx, 0, keepdims=False
    )

    def gather_slab(local_slab):
        return lax.all_gather(local_slab, "col", axis=1, tiled=True)

    def multiply(left_full):
        return jnp.dot(
            left_full,
            lax.all_gather(row_strips, "row", axis=0, tiled=True),
            preferred_element_type=jnp.float32,
        )

    partial_square = multiply(gather_slab(col_strips))
    square = lax.psum(partial_square, "depth").astype(jnp.bfloat16)
    square_strips = lax.dynamic_index_in_dim(
        square.reshape(rows_blk, groups, depth_n, strip_len), layer_idx, 2, keepdims=False
    ).reshape(rows_blk, groups * strip_len)
    partial_cube = multiply(gather_slab(square_strips))
    cube_sum = lax.psum_scatter(-2.0 * partial_cube, "depth", scatter_dimension=1, tiled=True)
    share_width = cols_blk // depth_n
    own_square = lax.dynamic_slice_in_dim(square, layer_idx * share_width, share_width, 1).astype(
        jnp.float32
    )
    return cube_sum + 3.0 * own_square


def dot(a, b):
    return jnp.dot(a, b, preferred_element_type=jnp.float32)


def dot_t(a, b):
    return lax.dot_general(a, b, (((1,), (1,)), ((), ())), preferred_element_type=jnp.float32)


def turned(a):
    return jnp.transpose(a)


def place():
    z, x, d = lax.axis_index("row"), lax.axis_index("col"), lax.axis_index("depth")
    return z, x, d, lax.div(d, 2), lax.rem(d, 2)


def picked(z, x):
    return lax.rem(z, 2) ^ lax.div(z, 2) ^ x


def received(slot, other):
    z, x, _, _, _ = place()
    away = x ^ other ^ lax.div(z, 2)
    if slot == 0:
        return 2, 1 + away
    if slot == 1:
        return 1 + 2 * away, 1 + 2 * away
    return 3, 1 + away


def lanes(s, half):
    return pl.ds(pl.multiple_of(s * half, half), half)


def put(columns, i, k, quarter):
    half = quarter.shape[0]
    columns[k, lanes(i, half)] = quarter
    columns[i, lanes(k, half)] = turned(quarter)


def put_strip(columns, other, y_dist, same_core, other_core):
    _, _, _, y, c = place()
    for slot in range(3):
        i, k = received(slot, other)
        for cc, quarter in ((c, same_core(slot)), (1 - c, other_core(slot))):
            put(columns, 2 * i + (y ^ y_dist), 2 * k + cc, quarter)


def put_row(row, columns, m, rows, piece):
    half = columns.shape[2]
    for h in range(2):
        part = piece[:, h * half : (h + 1) * half]
        row[lanes(rows, half), lanes(2 * m + h, half)] = part
        put(columns, rows, 2 * m + h, part)


def home():
    z, x, _, _, _ = place()
    return (x == lax.div(z, 2)).astype(jnp.int32)


def early_halves():
    _, _, _, y, _ = place()
    at_home = home()
    return 0, 1, (4 + y) * (1 - at_home) + 2 * at_home, (6 + y) * (1 - at_home) + 3 * at_home


def late_halves():
    _, _, _, y, _ = place()
    at_home = home()
    return (
        2 + 2 * at_home,
        3 + 2 * at_home,
        (5 - y) * (1 - at_home) + (6 + y) * at_home,
        (7 - y),
    )


def half_kernel(array, before, out, upper):
    del before
    out[...] = array[:, : out.shape[1]] if upper else array[:, out.shape[1] :]


def join_kernel(a, b, before, out):
    del before
    out[: a.shape[0]] = a[...]
    out[a.shape[0] :] = b[...]


def stack_kernel(a, b, c, out):
    for n, ref in enumerate((a, b, c)):
        out[n] = ref[...]


def fetch(source, out, sem):
    copy = pltpu.make_async_copy(source, out, sem)
    copy.start()
    copy.wait()


def half_row_kernel(density, before, out, sem):
    del before
    _, _, _, _, c = place()
    fetch(density.at[lanes(c, out.shape[0])], out, sem)


def third_kernel(density, before, out, sem):
    del before
    z, x, _, y, c = place()
    half = out.shape[0]
    fetch(density.at[lanes(y, half), lanes(2 * (1 - picked(z, x)) + c, half)], out, sem)


def first_kernel(own, own0, row, columns):
    z, x, _, y, c = place()
    blk, half = own.shape[0], columns.shape[2]
    for b in range(2):
        m = (2 * x + b) ^ z
        for h in range(2):
            part = own[:, (2 * b + h) * half : (2 * b + h + 1) * half]
            row[:, lanes(2 * m + h, half)] = part
            columns[2 * m + h, :blk] = part
            for g in range(2):
                columns[g, lanes(2 * m + h, half)] = turned(part[g * half : (g + 1) * half])
    for slot in range(3):
        i, k = received(slot, 0)
        put(columns, 2 * i + y, 2 * k + c, own0[slot])


def pass_kernel(a, before, out):
    del before
    out[...] = a[...]


def cross_kernel(a, b, before, out):
    del before
    _, _, _, _, c = place()

    @pl.when(c == 0)
    def _():
        out[...] = a[...]

    @pl.when(c == 1)
    def _():
        out[...] = b[...]


def middle_kernel(row_in, columns_in, near, far, own1, own2, own3, oth0, oth1, row, columns, square, partial):
    del row_in, columns_in
    z, x, _, y, c = place()
    blk, half = near.shape[1] // 2, columns.shape[2]
    for b in range(2):
        m = (2 * (1 - x) + b) ^ z
        put_row(row, columns, m, c, near[:, b * blk : (b + 1) * blk])
        put_row(row, columns, m, 1 - c, far[:, b * blk : (b + 1) * blk])
    for slot in range(3):
        i, k = received(slot, 0)
        put(columns, 2 * i + y, 2 * k + 1 - c, own1[slot])
    put_strip(columns, 0, 1, lambda s: own2[s], lambda s: own3[s])
    put_strip(columns, 1, 0, lambda s: oth0[s], lambda s: oth1[s])
    nothing = jnp.zeros((half, half), columns.dtype)
    for slot in range(3):
        i, k = received(slot, 1)
        for h in range(2):
            columns[2 * k + h, lanes(2 * i + 1 - y, half)] = nothing

            @pl.when(i != k)
            def _(i=i, k=k, h=h):
                columns[2 * i + 1 - y, lanes(2 * k + h, half)] = nothing

    for s in early_halves():
        square[:, lanes(s, half)] = dot(row[...], columns[s]).astype(square.dtype)
    for n, s in enumerate(late_halves()):
        partial[n] = dot(row[...], columns[s])


def add_last(row, columns, partial, last, cc):
    _, _, _, y, _ = place()
    half, s = columns.shape[2], wanted()
    quarters = [last[slot] for slot in range(3)]
    for slot, q in enumerate(quarters):
        i, k = received(slot, 1)
        there, across = 2 * i + 1 - y, 2 * k + cc

        @pl.when(across == s)
        def _(there=there, q=q):
            columns[s, lanes(there, half)] = q

        @pl.when(there == s)
        def _(across=across, q=q):
            columns[s, lanes(across, half)] = turned(q)

    two, one, three = quarters

    def rows(h):
        return row[:, lanes(h, half)]

    @pl.when(home() == 1)
    def _():
        partial[cc] += dot(rows(5 - y), two) + dot(rows(7 - y), three)
        partial[3 - (cc ^ y ^ 1)] += dot(rows(7 - y), one)
        partial[3] += dot_t(rows(4 + cc), three)

    @pl.when(home() == 0)
    def _():
        partial[cc] += dot(rows(5 - y), two) + dot(rows(3 - y), one) + dot(rows(7 - y), three)
        partial[2] += dot_t(rows(2 + cc), two)
        partial[3] += dot_t(rows(2 + cc), three)


def wanted():
    z, x, _, y, c = place()
    return 2 * ((2 * x + y) ^ z) + c


def finish_kernel(row, columns_in, partial_in, square, oth2, columns, partial, cube):
    del columns_in, partial_in
    half = columns.shape[2]
    add_last(row, columns, partial, oth2, place()[4])
    s = wanted()
    acc = None
    for h in early_halves():
        term = dot(square[:, lanes(h, half)], columns[s, lanes(h, half)])
        acc = term if acc is None else acc + term
    cube[...] = acc


def last_kernel(row, columns_in, square, partial_in, cube, oth3, out, columns, partial):
    del columns_in, partial_in
    half = columns.shape[2]
    add_last(row, columns, partial, oth3, 1 - place()[4])
    s = wanted()
    acc, own = cube[...], square[:, lanes(s, half)].astype(jnp.float32)
    for n, h in enumerate(late_halves()):
        part = partial[n].astype(square.dtype)
        own = jnp.where(h == s, part.astype(jnp.float32), own)
        acc += dot(part, columns[s, lanes(h, half)])
    out[...] = 3.0 * own - 2.0 * acc


def call(kernel, name, flops, args, outs, aliases=None, order_only=0, scratch=()):
    return pl.pallas_call(
        kernel,
        out_shape=outs,
        in_specs=[pl.BlockSpec(memory_space=pltpu.VMEM)] * (len(args) - order_only)
        + [pl.BlockSpec(memory_space=pl.ANY)] * order_only,
        out_specs=[pl.BlockSpec(memory_space=pltpu.VMEM)] * len(outs),
        scratch_shapes=scratch,
        input_output_aliases=aliases or {},
        compiler_params=pltpu.CompilerParams(vmem_limit_bytes=16 * MIB),
        cost_estimate=pl.CostEstimate(flops=flops, bytes_accessed=0, transcendentals=0),
        name=name,
    )(*args)


def after(value, *others):
    return lax.optimization_barrier((value, *others))[0]


def gathered(density):
    blk, half = density.shape[0], density.shape[0] // 2
    z, x, d, y, c = place()
    cube = blk**3

    def by_z(v, m):
        return lax.ppermute(v, "row", [(i, i ^ m) for i in range(lax.axis_size("row"))])

    def by_x(v):
        return lax.ppermute(v, "col", [(i, i ^ 1) for i in range(lax.axis_size("col"))])

    def by_depth(v, m):
        return lax.ppermute(v, "depth", [(i, i ^ m) for i in range(lax.axis_size("depth"))])

    def crossed(v):
        n = lax.axis_size("depth")
        pairs = [(p, p ^ 2 if p % 2 == 0 else p ^ n) for p in range(lax.axis_size("col") * n)]
        return lax.ppermute(v, ("col", "depth"), pairs)

    def quarter(array, k):
        return lax.dynamic_slice(array, (y * half, k * blk + c * half), (half, half))

    def shape(*dims, dtype=jnp.bfloat16):
        return jax.ShapeDtypeStruct(dims, dtype)

    row_shape = shape(blk, 4 * blk)
    columns_shape = shape(8, 4 * blk, half)
    pick = picked(z, x)
    sent = quarter(density, pick)
    two_away = by_z(sent, 2)
    half_row = call(
        half_row_kernel,
        "half_row",
        40 * cube,
        (density, sent),
        (shape(half, 2 * blk),),
        order_only=2,
        scratch=[pltpu.SemaphoreType.DMA],
    )[0]
    third = call(
        third_kernel,
        "third",
        20 * cube,
        (density, half_row),
        (shape(half, half),),
        order_only=2,
        scratch=[pltpu.SemaphoreType.DMA],
    )[0]
    near = by_x(half_row)
    three_away = by_z(third, 3)
    one_away = by_z(jnp.where(lax.div(z, 2) == x, sent, two_away), 1)
    far = by_depth(near, 1)
    own0 = call(
        stack_kernel,
        "stack",
        0,
        (two_away, one_away, three_away),
        (shape(3, half, half),),
    )[0]
    oth0, own2 = by_x(own0), by_depth(own0, 2)
    own1 = by_depth(own0, 1)
    row, columns = call(
        first_kernel, "first_blocks", 2 * cube, (density, own0), (row_shape, columns_shape)
    )
    quarters = shape(3, half, half)
    oth1 = by_depth(call(pass_kernel, "oth0", 0, (oth0, row), (quarters,), order_only=1)[0], 1)
    own3 = by_depth(call(pass_kernel, "own2", 0, (own2, row), (quarters,), order_only=1)[0], 1)
    diagonal = call(
        cross_kernel, "cross", 0, (oth0, own2, row), (shape(3, half, half),), order_only=1
    )[0]
    oth2 = crossed(diagonal)
    row, columns, square, partial = call(
        middle_kernel,
        "middle_blocks",
        30 * cube,
        (row, columns, near, far, own1, own2, own3, oth0, oth1),
        (row_shape, columns_shape, row_shape, shape(4, blk, half, dtype=jnp.float32)),
        {0: 0, 1: 1},
    )
    oth2, partial = lax.optimization_barrier((oth2, partial))
    oth3 = by_depth(oth2, 1)
    partial_shape = shape(4, blk, half, dtype=jnp.float32)
    out_shape = shape(blk, half, dtype=jnp.float32)
    columns, partial, early = call(
        finish_kernel,
        "finish_blocks",
        4 * cube,
        (row, columns, partial, square, oth2),
        (columns_shape, partial_shape, out_shape),
        {1: 0, 2: 1},
    )
    return call(
        last_kernel,
        "last_blocks",
        8 * cube,
        (row, columns, square, partial, early, oth3),
        (out_shape, columns_shape, partial_shape),
        {1: 1, 3: 2},
    )[0]


def solution(mesh):
    four_by_two = mesh.shape["row"] == mesh.shape["depth"] == 2 * mesh.shape["col"] == 4
    return jax.shard_map(
        gathered if four_by_two else split_products,
        mesh=mesh,
        in_specs=(P("row", "col"),),
        out_specs=P("row", ("col", "depth")),
        check_vma=False,
    )
```

```python
import functools

import jax
import jax.numpy as jnp
from jax import lax
from jax.experimental import pallas as pl
from jax.experimental.pallas import tpu as pltpu
from jax.sharding import PartitionSpec as P

MIB = 1024 * 1024


def split_products(density):
    rows_blk, cols_blk = density.shape
    depth_n = lax.axis_size("depth")
    strip_len = rows_blk // depth_n
    groups = cols_blk // rows_blk
    layer_idx = lax.axis_index("depth")
    col_strips = lax.dynamic_index_in_dim(
        density.reshape(rows_blk, groups, depth_n, strip_len), layer_idx, 2, keepdims=False
    ).reshape(rows_blk, groups * strip_len)
    row_strips = lax.dynamic_index_in_dim(
        density.reshape(depth_n, strip_len, cols_blk), layer_idx, 0, keepdims=False
    )

    def gather_slab(local_slab):
        return lax.all_gather(local_slab, "col", axis=1, tiled=True)

    def multiply(left_full):
        return jnp.dot(
            left_full,
            lax.all_gather(row_strips, "row", axis=0, tiled=True),
            preferred_element_type=jnp.float32,
        )

    partial_square = multiply(gather_slab(col_strips))
    square = lax.psum(partial_square, "depth").astype(jnp.bfloat16)
    square_strips = lax.dynamic_index_in_dim(
        square.reshape(rows_blk, groups, depth_n, strip_len), layer_idx, 2, keepdims=False
    ).reshape(rows_blk, groups * strip_len)
    partial_cube = multiply(gather_slab(square_strips))
    cube_sum = lax.psum_scatter(-2.0 * partial_cube, "depth", scatter_dimension=1, tiled=True)
    share_width = cols_blk // depth_n
    own_square = lax.dynamic_slice_in_dim(square, layer_idx * share_width, share_width, 1).astype(
        jnp.float32
    )
    return cube_sum + 3.0 * own_square


def dot(a, b):
    return jnp.dot(a, b, preferred_element_type=jnp.float32)


def dot_t(a, b):
    return lax.dot_general(a, b, (((1,), (1,)), ((), ())), preferred_element_type=jnp.float32)


def turned(a):
    return jnp.transpose(a)


def place():
    z, x, d = lax.axis_index("row"), lax.axis_index("col"), lax.axis_index("depth")
    return z, x, d, lax.div(d, 2), lax.rem(d, 2)


def picked(z, x):
    return lax.rem(z, 2) ^ lax.div(z, 2) ^ x


def received(slot, other):
    z, x, _, _, _ = place()
    away = x ^ other ^ lax.div(z, 2)
    if slot == 0:
        return 2, 1 + away
    if slot == 1:
        return 1 + 2 * away, 1 + 2 * away
    return 3, 1 + away


def lanes(s, half):
    return pl.ds(pl.multiple_of(s * half, half), half)


def put(columns, i, k, quarter):
    half = quarter.shape[0]
    columns[k, lanes(i, half)] = quarter
    columns[i, lanes(k, half)] = turned(quarter)


def put_strip(columns, other, y_dist, same_core, other_core):
    _, _, _, y, c = place()
    for slot in range(3):
        i, k = received(slot, other)
        for cc, quarter in ((c, same_core(slot)), (1 - c, other_core(slot))):
            put(columns, 2 * i + (y ^ y_dist), 2 * k + cc, quarter)


def put_row(row, columns, m, rows, piece):
    half = columns.shape[2]
    for h in range(2):
        part = piece[:, h * half : (h + 1) * half]
        row[lanes(rows, half), lanes(2 * m + h, half)] = part
        put(columns, rows, 2 * m + h, part)


def home():
    z, x, _, _, _ = place()
    return (x == lax.div(z, 2)).astype(jnp.int32)


def early_halves():
    _, _, _, y, _ = place()
    at_home = home()
    return 0, 1, (4 + y) * (1 - at_home) + 2 * at_home, (6 + y) * (1 - at_home) + 3 * at_home


def late_halves():
    _, _, _, y, _ = place()
    at_home = home()
    return (
        2 + 2 * at_home,
        3 + 2 * at_home,
        (5 - y) * (1 - at_home) + (6 + y) * at_home,
        (7 - y),
    )


def half_kernel(array, before, out, upper):
    del before
    out[...] = array[:, : out.shape[1]] if upper else array[:, out.shape[1] :]


def join_kernel(a, b, before, out):
    del before
    out[: a.shape[0]] = a[...]
    out[a.shape[0] :] = b[...]


def stack_kernel(a, b, c, out):
    for n, ref in enumerate((a, b, c)):
        out[n] = ref[...]


def fetch(source, out, sem):
    copy = pltpu.make_async_copy(source, out, sem)
    copy.start()
    copy.wait()


def half_row_kernel(density, before, out, sem):
    del before
    _, _, _, _, c = place()
    fetch(density.at[lanes(c, out.shape[0])], out, sem)


def third_kernel(density, before, out, sem):
    del before
    z, x, _, y, c = place()
    half = out.shape[0]
    fetch(density.at[lanes(y, half), lanes(2 * (1 - picked(z, x)) + c, half)], out, sem)


def first_kernel(own, own0, row, columns):
    z, x, _, y, c = place()
    blk, half = own.shape[0], columns.shape[2]
    for b in range(2):
        m = (2 * x + b) ^ z
        for h in range(2):
            part = own[:, (2 * b + h) * half : (2 * b + h + 1) * half]
            row[:, lanes(2 * m + h, half)] = part
            columns[2 * m + h, :blk] = part
            for g in range(2):
                columns[g, lanes(2 * m + h, half)] = turned(part[g * half : (g + 1) * half])
    for slot in range(3):
        i, k = received(slot, 0)
        put(columns, 2 * i + y, 2 * k + c, own0[slot])


def pass_kernel(a, before, out):
    del before
    out[...] = a[...]


def cross_kernel(a, b, before, out):
    del before
    _, _, _, _, c = place()

    @pl.when(c == 0)
    def _():
        out[...] = a[...]

    @pl.when(c == 1)
    def _():
        out[...] = b[...]


def middle_kernel(row_in, columns_in, near, far, own1, own2, own3, oth0, oth1, row, columns, square, partial):
    del row_in, columns_in
    z, x, _, y, c = place()
    blk, half = near.shape[1] // 2, columns.shape[2]
    for b in range(2):
        m = (2 * (1 - x) + b) ^ z
        put_row(row, columns, m, c, near[:, b * blk : (b + 1) * blk])
        put_row(row, columns, m, 1 - c, far[:, b * blk : (b + 1) * blk])
    for slot in range(3):
        i, k = received(slot, 0)
        put(columns, 2 * i + y, 2 * k + 1 - c, own1[slot])
    put_strip(columns, 0, 1, lambda s: own2[s], lambda s: own3[s])
    put_strip(columns, 1, 0, lambda s: oth0[s], lambda s: oth1[s])
    nothing = jnp.zeros((half, half), columns.dtype)
    for slot in range(3):
        i, k = received(slot, 1)
        for h in range(2):
            columns[2 * k + h, lanes(2 * i + 1 - y, half)] = nothing

            @pl.when(i != k)
            def _(i=i, k=k, h=h):
                columns[2 * i + 1 - y, lanes(2 * k + h, half)] = nothing

    for s in early_halves():
        square[:, lanes(s, half)] = dot(row[...], columns[s]).astype(square.dtype)
    for n, s in enumerate(late_halves()):
        partial[n] = dot(row[...], columns[s])


def add_last(row, columns, partial, last, cc):
    _, _, _, y, _ = place()
    half, s = columns.shape[2], wanted()
    quarters = [last[slot] for slot in range(3)]
    for slot, q in enumerate(quarters):
        i, k = received(slot, 1)
        there, across = 2 * i + 1 - y, 2 * k + cc

        @pl.when(across == s)
        def _(there=there, q=q):
            columns[s, lanes(there, half)] = q

        @pl.when(there == s)
        def _(across=across, q=q):
            columns[s, lanes(across, half)] = turned(q)

    two, one, three = quarters

    def rows(h):
        return row[:, lanes(h, half)]

    @pl.when(home() == 1)
    def _():
        partial[cc] += dot(rows(5 - y), two) + dot(rows(7 - y), three)
        partial[3 - (cc ^ y ^ 1)] += dot(rows(7 - y), one)
        partial[3] += dot_t(rows(4 + cc), three)

    @pl.when(home() == 0)
    def _():
        partial[cc] += dot(rows(5 - y), two) + dot(rows(3 - y), one) + dot(rows(7 - y), three)
        partial[2] += dot_t(rows(2 + cc), two)
        partial[3] += dot_t(rows(2 + cc), three)


def wanted():
    z, x, _, y, c = place()
    return 2 * ((2 * x + y) ^ z) + c


def finish_kernel(row, columns_in, partial_in, square, oth2, columns, partial, cube):
    del columns_in, partial_in
    half = columns.shape[2]
    add_last(row, columns, partial, oth2, place()[4])
    s = wanted()
    acc = None
    for h in early_halves():
        term = dot(square[:, lanes(h, half)], columns[s, lanes(h, half)])
        acc = term if acc is None else acc + term
    c = place()[4]
    h = late_halves()[0] + c
    cube[...] = acc + dot(partial[c].astype(square.dtype), columns[s, lanes(h, half)])


def last_kernel(row, columns_in, square, partial_in, cube, oth3, out, columns, partial):
    del columns_in, partial_in
    half = columns.shape[2]
    add_last(row, columns, partial, oth3, 1 - place()[4])
    s = wanted()
    acc, own = cube[...], square[:, lanes(s, half)].astype(jnp.float32)
    c, late = place()[4], late_halves()
    own = jnp.where(late[0] + c == s, partial[c].astype(square.dtype).astype(jnp.float32), own)
    for n, h in ((1 - c, late[0] + 1 - c), (2, late[2]), (3, late[3])):
        part = partial[n].astype(square.dtype)
        own = jnp.where(h == s, part.astype(jnp.float32), own)
        acc += dot(part, columns[s, lanes(h, half)])
    out[...] = 3.0 * own - 2.0 * acc


def call(kernel, name, flops, args, outs, aliases=None, order_only=0, scratch=()):
    return pl.pallas_call(
        kernel,
        out_shape=outs,
        in_specs=[pl.BlockSpec(memory_space=pltpu.VMEM)] * (len(args) - order_only)
        + [pl.BlockSpec(memory_space=pl.ANY)] * order_only,
        out_specs=[pl.BlockSpec(memory_space=pltpu.VMEM)] * len(outs),
        scratch_shapes=scratch,
        input_output_aliases=aliases or {},
        compiler_params=pltpu.CompilerParams(vmem_limit_bytes=16 * MIB),
        cost_estimate=pl.CostEstimate(flops=flops, bytes_accessed=0, transcendentals=0),
        name=name,
    )(*args)


def after(value, *others):
    return lax.optimization_barrier((value, *others))[0]


def gathered(density):
    blk, half = density.shape[0], density.shape[0] // 2
    z, x, d, y, c = place()
    cube = blk**3

    def by_z(v, m):
        return lax.ppermute(v, "row", [(i, i ^ m) for i in range(lax.axis_size("row"))])

    def by_x(v):
        return lax.ppermute(v, "col", [(i, i ^ 1) for i in range(lax.axis_size("col"))])

    def by_depth(v, m):
        return lax.ppermute(v, "depth", [(i, i ^ m) for i in range(lax.axis_size("depth"))])

    def crossed(v):
        n = lax.axis_size("depth")
        pairs = [(p, p ^ 2 if p % 2 == 0 else p ^ n) for p in range(lax.axis_size("col") * n)]
        return lax.ppermute(v, ("col", "depth"), pairs)

    def quarter(array, k):
        return lax.dynamic_slice(array, (y * half, k * blk + c * half), (half, half))

    def shape(*dims, dtype=jnp.bfloat16):
        return jax.ShapeDtypeStruct(dims, dtype)

    row_shape = shape(blk, 4 * blk)
    columns_shape = shape(8, 4 * blk, half)
    pick = picked(z, x)
    sent = quarter(density, pick)
    two_away = by_z(sent, 2)
    half_row = call(
        half_row_kernel,
        "half_row",
        40 * cube,
        (density, sent),
        (shape(half, 2 * blk),),
        order_only=2,
        scratch=[pltpu.SemaphoreType.DMA],
    )[0]
    third = call(
        third_kernel,
        "third",
        20 * cube,
        (density, half_row),
        (shape(half, half),),
        order_only=2,
        scratch=[pltpu.SemaphoreType.DMA],
    )[0]
    near = by_x(half_row)
    three_away = by_z(third, 3)
    one_away = by_z(jnp.where(lax.div(z, 2) == x, sent, two_away), 1)
    far = by_depth(near, 1)
    own0 = call(
        stack_kernel,
        "stack",
        0,
        (two_away, one_away, three_away),
        (shape(3, half, half),),
    )[0]
    oth0, own2 = by_x(own0), by_depth(own0, 2)
    own1 = by_depth(own0, 1)
    row, columns = call(
        first_kernel, "first_blocks", 2 * cube, (density, own0), (row_shape, columns_shape)
    )
    quarters = shape(3, half, half)
    oth1 = by_depth(call(pass_kernel, "oth0", 0, (oth0, row), (quarters,), order_only=1)[0], 1)
    own3 = by_depth(call(pass_kernel, "own2", 0, (own2, row), (quarters,), order_only=1)[0], 1)
    diagonal = call(
        cross_kernel, "cross", 0, (oth0, own2, row), (shape(3, half, half),), order_only=1
    )[0]
    oth2 = crossed(diagonal)
    row, columns, square, partial = call(
        middle_kernel,
        "middle_blocks",
        30 * cube,
        (row, columns, near, far, own1, own2, own3, oth0, oth1),
        (row_shape, columns_shape, row_shape, shape(4, blk, half, dtype=jnp.float32)),
        {0: 0, 1: 1},
    )
    oth2, partial = lax.optimization_barrier((oth2, partial))
    oth3 = by_depth(oth2, 1)
    partial_shape = shape(4, blk, half, dtype=jnp.float32)
    out_shape = shape(blk, half, dtype=jnp.float32)
    columns, partial, early = call(
        finish_kernel,
        "finish_blocks",
        4 * cube,
        (row, columns, partial, square, oth2),
        (columns_shape, partial_shape, out_shape),
        {1: 0, 2: 1},
    )
    return call(
        last_kernel,
        "last_blocks",
        8 * cube,
        (row, columns, square, partial, early, oth3),
        (out_shape, columns_shape, partial_shape),
        {1: 1, 3: 2},
    )[0]


def solution(mesh):
    four_by_two = mesh.shape["row"] == mesh.shape["depth"] == 2 * mesh.shape["col"] == 4
    return jax.shard_map(
        gathered if four_by_two else split_products,
        mesh=mesh,
        in_specs=(P("row", "col"),),
        out_specs=P("row", ("col", "depth")),
        check_vma=False,
    )
```

```python
import functools

import jax
import jax.numpy as jnp
from jax import lax
from jax.experimental import pallas as pl
from jax.experimental.pallas import tpu as pltpu
from jax.sharding import PartitionSpec as P

MIB = 1024 * 1024


def split_products(density):
    rows_blk, cols_blk = density.shape
    depth_n = lax.axis_size("depth")
    strip_len = rows_blk // depth_n
    groups = cols_blk // rows_blk
    layer_idx = lax.axis_index("depth")
    col_strips = lax.dynamic_index_in_dim(
        density.reshape(rows_blk, groups, depth_n, strip_len), layer_idx, 2, keepdims=False
    ).reshape(rows_blk, groups * strip_len)
    row_strips = lax.dynamic_index_in_dim(
        density.reshape(depth_n, strip_len, cols_blk), layer_idx, 0, keepdims=False
    )

    def gather_slab(local_slab):
        return lax.all_gather(local_slab, "col", axis=1, tiled=True)

    def multiply(left_full):
        return jnp.dot(
            left_full,
            lax.all_gather(row_strips, "row", axis=0, tiled=True),
            preferred_element_type=jnp.float32,
        )

    partial_square = multiply(gather_slab(col_strips))
    square = lax.psum(partial_square, "depth").astype(jnp.bfloat16)
    square_strips = lax.dynamic_index_in_dim(
        square.reshape(rows_blk, groups, depth_n, strip_len), layer_idx, 2, keepdims=False
    ).reshape(rows_blk, groups * strip_len)
    partial_cube = multiply(gather_slab(square_strips))
    cube_sum = lax.psum_scatter(-2.0 * partial_cube, "depth", scatter_dimension=1, tiled=True)
    share_width = cols_blk // depth_n
    own_square = lax.dynamic_slice_in_dim(square, layer_idx * share_width, share_width, 1).astype(
        jnp.float32
    )
    return cube_sum + 3.0 * own_square


def dot(a, b):
    return jnp.dot(a, b, preferred_element_type=jnp.float32)


def dot_t(a, b):
    return lax.dot_general(a, b, (((1,), (1,)), ((), ())), preferred_element_type=jnp.float32)


def turned(a):
    return jnp.transpose(a)


def place():
    z, x, d = lax.axis_index("row"), lax.axis_index("col"), lax.axis_index("depth")
    return z, x, d, lax.div(d, 2), lax.rem(d, 2)


def picked(z, x):
    return lax.rem(z, 2) ^ lax.div(z, 2) ^ x


def received(slot, other):
    z, x, _, _, _ = place()
    away = x ^ other ^ lax.div(z, 2)
    if slot == 0:
        return 2, 1 + away
    if slot == 1:
        return 1 + 2 * away, 1 + 2 * away
    return 3, 1 + away


def lanes(s, half):
    return pl.ds(pl.multiple_of(s * half, half), half)


def put(columns, i, k, quarter):
    half = quarter.shape[0]
    columns[k, lanes(i, half)] = quarter
    columns[i, lanes(k, half)] = turned(quarter)


def put_strip(columns, other, y_dist, same_core, other_core):
    _, _, _, y, c = place()
    for slot in range(3):
        i, k = received(slot, other)
        for cc, quarter in ((c, same_core(slot)), (1 - c, other_core(slot))):
            put(columns, 2 * i + (y ^ y_dist), 2 * k + cc, quarter)


def put_row(row, columns, m, rows, piece):
    half = columns.shape[2]
    for h in range(2):
        part = piece[:, h * half : (h + 1) * half]
        row[lanes(rows, half), lanes(2 * m + h, half)] = part
        put(columns, rows, 2 * m + h, part)


def home():
    z, x, _, _, _ = place()
    return (x == lax.div(z, 2)).astype(jnp.int32)


def early_halves():
    _, _, _, y, _ = place()
    at_home = home()
    return 0, 1, (4 + y) * (1 - at_home) + 2 * at_home, (6 + y) * (1 - at_home) + 3 * at_home


def late_halves():
    _, _, _, y, _ = place()
    at_home = home()
    return (
        2 + 2 * at_home,
        3 + 2 * at_home,
        (5 - y) * (1 - at_home) + (6 + y) * at_home,
        (7 - y),
    )


def half_kernel(array, before, out, upper):
    del before
    out[...] = array[:, : out.shape[1]] if upper else array[:, out.shape[1] :]


def join_kernel(a, b, before, out):
    del before
    out[: a.shape[0]] = a[...]
    out[a.shape[0] :] = b[...]


def stack_kernel(a, b, c, out):
    for n, ref in enumerate((a, b, c)):
        out[n] = ref[...]


def fetch(source, out, sem):
    copy = pltpu.make_async_copy(source, out, sem)
    copy.start()
    copy.wait()


def half_row_kernel(density, before, out, sem):
    del before
    _, _, _, _, c = place()
    fetch(density.at[lanes(c, out.shape[0])], out, sem)


def third_kernel(density, before, out, sem):
    del before
    z, x, _, y, c = place()
    half = out.shape[0]
    fetch(density.at[lanes(y, half), lanes(2 * (1 - picked(z, x)) + c, half)], out, sem)


def first_kernel(own, own0, near, row, columns):
    z, x, _, y, c = place()
    blk, half = own.shape[0], columns.shape[2]
    for b in range(2):
        m = (2 * x + b) ^ z
        for h in range(2):
            part = own[:, (2 * b + h) * half : (2 * b + h + 1) * half]
            row[:, lanes(2 * m + h, half)] = part
            columns[2 * m + h, :blk] = part
            for g in range(2):
                columns[g, lanes(2 * m + h, half)] = turned(part[g * half : (g + 1) * half])
    for b in range(2):
        put_row(row, columns, (2 * (1 - x) + b) ^ z, c, near[:, b * blk : (b + 1) * blk])
    for slot in range(3):
        i, k = received(slot, 0)
        put(columns, 2 * i + y, 2 * k + c, own0[slot])


def pass_kernel(a, before, out):
    del before
    out[...] = a[...]


def cross_kernel(a, b, before, out):
    del before
    _, _, _, _, c = place()

    @pl.when(c == 0)
    def _():
        out[...] = a[...]

    @pl.when(c == 1)
    def _():
        out[...] = b[...]


def middle_kernel(row_in, columns_in, far, own1, own2, own3, oth0, oth1, row, columns, square, partial):
    del row_in, columns_in
    z, x, _, y, c = place()
    blk, half = far.shape[1] // 2, columns.shape[2]
    for b in range(2):
        m = (2 * (1 - x) + b) ^ z
        put_row(row, columns, m, 1 - c, far[:, b * blk : (b + 1) * blk])
    for slot in range(3):
        i, k = received(slot, 0)
        put(columns, 2 * i + y, 2 * k + 1 - c, own1[slot])
    put_strip(columns, 0, 1, lambda s: own2[s], lambda s: own3[s])
    put_strip(columns, 1, 0, lambda s: oth0[s], lambda s: oth1[s])
    nothing = jnp.zeros((half, half), columns.dtype)
    for slot in range(3):
        i, k = received(slot, 1)
        for h in range(2):
            columns[2 * k + h, lanes(2 * i + 1 - y, half)] = nothing

            @pl.when(i != k)
            def _(i=i, k=k, h=h):
                columns[2 * i + 1 - y, lanes(2 * k + h, half)] = nothing

    for s in early_halves():
        square[:, lanes(s, half)] = dot(row[...], columns[s]).astype(square.dtype)
    for n, s in enumerate(late_halves()):
        partial[n] = dot(row[...], columns[s])


def add_last(row, columns, partial, last, cc):
    _, _, _, y, _ = place()
    half, s = columns.shape[2], wanted()
    quarters = [last[slot] for slot in range(3)]
    for slot, q in enumerate(quarters):
        i, k = received(slot, 1)
        there, across = 2 * i + 1 - y, 2 * k + cc

        @pl.when(across == s)
        def _(there=there, q=q):
            columns[s, lanes(there, half)] = q

        @pl.when(there == s)
        def _(across=across, q=q):
            columns[s, lanes(across, half)] = turned(q)

    two, one, three = quarters

    def rows(h):
        return row[:, lanes(h, half)]

    @pl.when(home() == 1)
    def _():
        partial[cc] += dot(rows(5 - y), two) + dot(rows(7 - y), three)
        partial[3 - (cc ^ y ^ 1)] += dot(rows(7 - y), one)
        partial[3] += dot_t(rows(4 + cc), three)

    @pl.when(home() == 0)
    def _():
        partial[cc] += dot(rows(5 - y), two) + dot(rows(3 - y), one) + dot(rows(7 - y), three)
        partial[2] += dot_t(rows(2 + cc), two)
        partial[3] += dot_t(rows(2 + cc), three)


def wanted():
    z, x, _, y, c = place()
    return 2 * ((2 * x + y) ^ z) + c


def finish_kernel(row, columns_in, partial_in, square, oth2, columns, partial, cube):
    del columns_in, partial_in
    half = columns.shape[2]
    add_last(row, columns, partial, oth2, place()[4])
    s = wanted()
    acc = None
    for h in early_halves():
        term = dot(square[:, lanes(h, half)], columns[s, lanes(h, half)])
        acc = term if acc is None else acc + term
    cube[...] = acc


def last_kernel(row, columns_in, square, partial_in, cube, oth3, out, columns, partial):
    del columns_in, partial_in
    half = columns.shape[2]
    add_last(row, columns, partial, oth3, 1 - place()[4])
    s = wanted()
    acc, own = cube[...], square[:, lanes(s, half)].astype(jnp.float32)
    for n, h in enumerate(late_halves()):
        part = partial[n].astype(square.dtype)
        own = jnp.where(h == s, part.astype(jnp.float32), own)
        acc += dot(part, columns[s, lanes(h, half)])
    out[...] = 3.0 * own - 2.0 * acc


def call(kernel, name, flops, args, outs, aliases=None, order_only=0, scratch=()):
    return pl.pallas_call(
        kernel,
        out_shape=outs,
        in_specs=[pl.BlockSpec(memory_space=pltpu.VMEM)] * (len(args) - order_only)
        + [pl.BlockSpec(memory_space=pl.ANY)] * order_only,
        out_specs=[pl.BlockSpec(memory_space=pltpu.VMEM)] * len(outs),
        scratch_shapes=scratch,
        input_output_aliases=aliases or {},
        compiler_params=pltpu.CompilerParams(vmem_limit_bytes=16 * MIB),
        cost_estimate=pl.CostEstimate(flops=flops, bytes_accessed=0, transcendentals=0),
        name=name,
    )(*args)


def after(value, *others):
    return lax.optimization_barrier((value, *others))[0]


def gathered(density):
    blk, half = density.shape[0], density.shape[0] // 2
    z, x, d, y, c = place()
    cube = blk**3

    def by_z(v, m):
        return lax.ppermute(v, "row", [(i, i ^ m) for i in range(lax.axis_size("row"))])

    def by_x(v):
        return lax.ppermute(v, "col", [(i, i ^ 1) for i in range(lax.axis_size("col"))])

    def by_depth(v, m):
        return lax.ppermute(v, "depth", [(i, i ^ m) for i in range(lax.axis_size("depth"))])

    def crossed(v):
        n = lax.axis_size("depth")
        pairs = [(p, p ^ 2 if p % 2 == 0 else p ^ n) for p in range(lax.axis_size("col") * n)]
        return lax.ppermute(v, ("col", "depth"), pairs)

    def quarter(array, k):
        return lax.dynamic_slice(array, (y * half, k * blk + c * half), (half, half))

    def shape(*dims, dtype=jnp.bfloat16):
        return jax.ShapeDtypeStruct(dims, dtype)

    row_shape = shape(blk, 4 * blk)
    columns_shape = shape(8, 4 * blk, half)
    pick = picked(z, x)
    sent = quarter(density, pick)
    two_away = by_z(sent, 2)
    half_row = call(
        half_row_kernel,
        "half_row",
        40 * cube,
        (density, sent),
        (shape(half, 2 * blk),),
        order_only=2,
        scratch=[pltpu.SemaphoreType.DMA],
    )[0]
    third = call(
        third_kernel,
        "third",
        20 * cube,
        (density, half_row),
        (shape(half, half),),
        order_only=2,
        scratch=[pltpu.SemaphoreType.DMA],
    )[0]
    near = by_x(half_row)
    three_away = by_z(third, 3)
    one_away = by_z(jnp.where(lax.div(z, 2) == x, sent, two_away), 1)
    far = by_depth(near, 1)
    own0 = call(
        stack_kernel,
        "stack",
        0,
        (two_away, one_away, three_away),
        (shape(3, half, half),),
    )[0]
    oth0, own2 = by_x(own0), by_depth(own0, 2)
    own1 = by_depth(own0, 1)
    row, columns = call(
        first_kernel, "first_blocks", 2 * cube, (density, own0, near), (row_shape, columns_shape)
    )
    quarters = shape(3, half, half)
    oth1 = by_depth(call(pass_kernel, "oth0", 0, (oth0, row), (quarters,), order_only=1)[0], 1)
    own3 = by_depth(call(pass_kernel, "own2", 0, (own2, row), (quarters,), order_only=1)[0], 1)
    diagonal = call(
        cross_kernel, "cross", 0, (oth0, own2, row), (shape(3, half, half),), order_only=1
    )[0]
    oth2 = crossed(diagonal)
    row, columns, square, partial = call(
        middle_kernel,
        "middle_blocks",
        30 * cube,
        (row, columns, far, own1, own2, own3, oth0, oth1),
        (row_shape, columns_shape, row_shape, shape(4, blk, half, dtype=jnp.float32)),
        {0: 0, 1: 1},
    )
    oth2, partial = lax.optimization_barrier((oth2, partial))
    oth3 = by_depth(oth2, 1)
    partial_shape = shape(4, blk, half, dtype=jnp.float32)
    out_shape = shape(blk, half, dtype=jnp.float32)
    columns, partial, early = call(
        finish_kernel,
        "finish_blocks",
        4 * cube,
        (row, columns, partial, square, oth2),
        (columns_shape, partial_shape, out_shape),
        {1: 0, 2: 1},
    )
    return call(
        last_kernel,
        "last_blocks",
        8 * cube,
        (row, columns, square, partial, early, oth3),
        (out_shape, columns_shape, partial_shape),
        {1: 1, 3: 2},
    )[0]


def solution(mesh):
    four_by_two = mesh.shape["row"] == mesh.shape["depth"] == 2 * mesh.shape["col"] == 4
    return jax.shard_map(
        gathered if four_by_two else split_products,
        mesh=mesh,
        in_specs=(P("row", "col"),),
        out_specs=P("row", ("col", "depth")),
        check_vma=False,
    )
```
